32 devices in a mesh: groups: 2 (over x), wide: 16 (over z, y, core).
Axes of the slice: x: 2, y: 2, z: 4, core: 2. Of those that a mesh axis runs over, the one named last changes fastest.
Arguments:
- features: float32 [4, 32, 16, 256], P('groups', 'wide'), parts along dimension 0, may hold values from -6 to 6
- first_weight: float32 [3, 3, 256, 256], replicated, may hold values from -0.125 to 0.125
- down_weight: float32 [2, 2, 256, 1024], replicated, may hold values from -0.1875 to 0.1875
- inner_weight: float32 [1, 3, 3, 1024, 1024], P(None, None, None, None, 'wide'), may hold values from -0.0625 to 0.0625
- outer_weight: float32 [1, 3, 3, 1024, 1024], P(None, None, None, None, 'wide'), may hold values from -0.0625 to 0.0625
Outputs:
- refined: float32 [4, 16, 8, 1024], P('groups', None, None, 'wide'), parts along dimension 0
The draws below stay inside these ranges and needn't reach their ends.
There are 2 independent parts, one for each index of `groups`. The reference program is written for one: setup_inputs(seed, part) draws one part's arguments, and reference() takes and returns one part's arrays. A program takes and returns all parts, laid end to end along the dimension named above; an argument that names none is the same for every part. Nothing has to cross between parts.
All inputs are finite; a program needn't handle non-finite values.
Results may differ from the reference program's by a relative error of at most 0.00013.
Values sent between devices are 32-bit elements; how exact they have to be, the bound alone decides.
A program may use at most 64 MiB of HBM per device.

```python
import jax
import jax.numpy as jnp
from jax import lax

CH = 256
F = 1024
SECTIONS = 1
MB = 2
COLS = 16
ROWS = 32


def block_scale(stream_key, shape, shards, smallest, high):
    level = 1.0
    for dim, shards_of in shards:
        steps = jax.random.uniform(jax.random.fold_in(jax.random.fold_in(stream_key, 6), dim), (shards_of,), jnp.float32, smallest / len(shards), high / len(shards))
        level = level * jnp.repeat(jnp.exp(steps), shape[dim] // shards_of).reshape((-1,) + (1,) * (len(shape) - 1 - dim))
    return level


def scatter_about(stream_key, shape, deviation, reach, cuts=(), kind=jnp.bfloat16):
    values = deviation * jax.random.normal(stream_key, shape, jnp.float32)
    if cuts:
        values = values * block_scale(stream_key, shape, cuts, -0.22, 0.18)
    return jnp.clip(values, -reach, reach).astype(kind)


def setup_inputs(seed: int = 0, part: int = 0) -> dict:
    key_of = jax.random.split(jax.random.key(seed), 6)
    part_splits = jax.random.split(jax.random.fold_in(key_of[5], part), 6)
    features = scatter_about(part_splits[0], (MB, ROWS, COLS, CH), 1.0, 6.0, ((1, 16),), jnp.float32)
    first_weight = scatter_about(key_of[1], (3, 3, CH, CH), (9 * CH) ** -0.5, 0.125, (), jnp.float32)
    down_weight = scatter_about(key_of[2], (2, 2, CH, F), (4 * CH) ** -0.5, 0.1875, (), jnp.float32)
    inner_weight = scatter_about(key_of[3], (SECTIONS, 3, 3, F, F), (9 * F) ** -0.5, 0.0625, ((4, 16),), jnp.float32)
    outer_weight = scatter_about(key_of[4], (SECTIONS, 3, 3, F, F), (9 * F) ** -0.5, 0.0625, ((4, 16),), jnp.float32)
    return dict(features=features, first_weight=first_weight, down_weight=down_weight, inner_weight=inner_weight, outer_weight=outer_weight)


def convolve(feature_map, kernel, layout, strides, padding):
    return lax.conv_general_dilated(feature_map, kernel, strides, padding, dimension_numbers=("NHWC", layout, "NHWC"), precision=lax.Precision.HIGHEST)


def reference(features, first_weight, down_weight, inner_weight, outer_weight):
    activated = jax.nn.relu(convolve(features, first_weight, "HWIO", (1, 1), "SAME"))
    current = convolve(activated, down_weight, "HWIO", (2, 2), "VALID")
    for section in range(SECTIONS):
        inner = jax.nn.relu(convolve(current, inner_weight[section], "HWOI", (1, 1), "SAME"))
        current = jax.nn.relu(current + convolve(inner, outer_weight[section], "HWIO", (1, 1), "SAME"))
    return current
```

```python
import functools

import jax
import jax.numpy as jnp
from jax import lax
from jax.experimental import pallas as pl
from jax.experimental.pallas import tpu as pltpu
from jax.sharding import PartitionSpec as P


def extended_2(shard, sides, width):
    for axis, dim in sides:
        size, length = (lax.axis_size(axis), shard.shape[dim])
        up = [(i, (i + 1) % size) for i in range(size - 1)]
        down = [(j, i) for i, j in up]
        last = lax.slice_in_dim(shard, length - width, length, axis=dim)
        first = lax.slice_in_dim(shard, 0, width, axis=dim)
        before = lax.ppermute(last, axis, up)
        after = lax.ppermute(first, axis, down)
        shard = jnp.concatenate([before, shard, after], axis=dim)
    return shard


def partner_2(block, axis, distance):
    count = lax.axis_size(axis)
    route = []
    for low in range(count):
        high = low | 1 << distance
        if high != low and high < count:
            route += [(low, high), (high, low)]
    return lax.ppermute(block, axis, route)


def convolve(feature_map, kernel, layout, strides, padding):
    return lax.conv_general_dilated(
        feature_map,
        kernel,
        strides,
        padding,
        dimension_numbers=("NHWC", layout, "NHWC"),
        precision=lax.Precision.HIGHEST,
    )


def device_bit(bit_number):
    return lax.axis_index("wide") >> bit_number & 1


def spatial(local_rows, first_weight, down_weight):
    extended = extended_2(local_rows, (("wide", 1),), 1)
    activated = jax.nn.relu(convolve(extended, first_weight, "HWIO", (1, 1), [(0, 0), (1, 1)]))
    return convolve(activated, down_weight, "HWIO", (2, 2), "VALID")


def weight_blocks(stacked, grid_size, low_bits):
    leading = stacked.shape[:-2]
    width = stacked.shape[-2]
    narrow = stacked.shape[-1]
    slots = jnp.moveaxis(stacked.reshape(leading + (grid_size, width // grid_size, narrow)), -3, 0)
    remainder = slots.shape[1:]
    for bit_number in low_bits:
        paired = slots.reshape((grid_size >> bit_number + 1, 2, 1 << bit_number) + remainder)
        lower = paired[:, 0]
        upper = paired[:, 1]
        first_half = device_bit(bit_number) == 0
        outgoing = jnp.where(first_half, upper, lower)
        keeping = jnp.where(first_half, lower, upper)
        incoming = partner_2(outgoing, "wide", bit_number)
        merged = jnp.stack(
            [jnp.where(first_half, keeping, incoming), jnp.where(first_half, incoming, keeping)], 1
        )
        slots = merged.reshape((grid_size,) + remainder)
    joined = jnp.moveaxis(slots, 0, -2)
    return joined.reshape(leading + (width // grid_size, grid_size * narrow))


def channel_pieces(piece, low_bits):
    for bit_number in low_bits:
        partner = partner_2(piece, "wide", bit_number)
        first_half = device_bit(bit_number) == 0
        piece = jnp.where(
            first_half, jnp.concatenate([piece, partner], 3), jnp.concatenate([partner, piece], 3)
        )
    return piece


def group_total(partial_value, bit_list):
    for bit_number in bit_list:
        partial_value = partial_value + partner_2(partial_value, "wide", bit_number)
    return partial_value


def body(features, first_weight, down_weight, inner_weight, outer_weight):
    total_bits = lax.axis_size("wide").bit_length() - 1
    half_bits = total_bits // 2
    grid_size = 1 << half_bits
    low_bits = list(range(half_bits))
    high_bits = list(range(half_bits, total_bits))
    channels = down_weight.shape[3]
    stacked = weight_blocks(jnp.stack([inner_weight, outer_weight], 0), grid_size, low_bits)
    reduced = spatial(features, first_weight, down_weight)
    current = channel_pieces(
        lax.all_to_all(reduced, "wide", split_axis=3, concat_axis=1, tiled=True), low_bits
    )
    kernel_in = stacked[0, 0]
    kernel_out = stacked[1, 0]
    partial_value = convolve(current, kernel_in, "HWOI", (1, 1), "SAME")
    hidden = jax.nn.relu(group_total(partial_value, high_bits))
    partial_value = convolve(hidden, kernel_out, "HWIO", (1, 1), "SAME")
    current = jax.nn.relu(current + group_total(partial_value, low_bits))
    own_count = channels // lax.axis_size("wide")
    offset = lax.axis_index("wide") % grid_size * own_count
    return lax.dynamic_slice_in_dim(current, offset, own_count, 3)

MESH = pl.DeviceIdType.MESH
F32 = jnp.float32
BF16 = jnp.bfloat16


def halves(value):
    high = value.astype(BF16)
    return high, (value - high.astype(F32)).astype(BF16)


def dot(a, b):
    return jnp.dot(a, b, preferred_element_type=F32)


def fused(
    wide,
    feat_hbm, first_hbm, down_hbm, inner_hbm, outer_hbm, out_ref,
    feat, first, down, inner, outer,
    first_hi, first_lo, down_hi, down_lo, inner_hi, inner_lo, outer_all,
    halo, ext, cols1, act, cols2, red, gathered, ext2, cols3,
    part, scat, hid, taps_out, mine, theirs,
    local_sem, halo_send, halo_recv, weight_send, weight_recv,
    a2a_send, a2a_recv, rs_send, rs_recv, ag_send, ag_recv, fin_send, fin_recv,
):
    me = lax.axis_index("wide")
    core = lax.rem(me, 2)
    chip = lax.div(me, 2)
    mate = me + 1 - 2 * core
    chips = wide // 2
    fields, rows, columns, ch = feat.shape
    own = inner.shape[2]
    half = inner.shape[3]
    pair = 2 * own
    out_cols = columns // 2
    field_pos = wide * out_cols
    block = inner_hi.shape[2]
    per_block = block // own
    blocks = half // block

    def remote(src, dst, send, recv, device):
        return pltpu.make_async_remote_copy(
            src_ref=src, dst_ref=dst, send_sem=send, recv_sem=recv,
            device_id={"wide": device}, device_id_type=MESH,
        )

    my_half = pl.ds(pl.multiple_of(core * half, half), half)
    mate_half = pl.ds(pl.multiple_of((1 - core) * half, half), half)
    local = [
        pltpu.make_async_copy(feat_hbm, feat, local_sem.at[0]),
        pltpu.make_async_copy(first_hbm, first, local_sem.at[1]),
        pltpu.make_async_copy(down_hbm, down, local_sem.at[2]),
        pltpu.make_async_copy(inner_hbm.at[:, :, my_half], inner.at[core], local_sem.at[3]),
        pltpu.make_async_copy(outer_hbm.at[:, :, my_half], outer.at[core], local_sem.at[4]),
    ]
    for copy in local:
        copy.start()

    barrier = pltpu.get_barrier_semaphore()

    def greet(k, carry):
        pl.semaphore_signal(
            barrier, inc=1, device_id={"wide": lax.rem(me + k, wide)}, device_id_type=MESH
        )
        return carry

    lax.fori_loop(1, wide, greet, 0)
    ext[...] = jnp.zeros_like(ext)
    ext2[...] = jnp.zeros_like(ext2)
    local[0].wait()
    pl.semaphore_wait(barrier, wide - 1)

    down_copy = remote(feat.at[:, rows - 1], halo.at[0], halo_send.at[0], halo_recv.at[0], me + 1)
    up_copy = remote(feat.at[:, 0], halo.at[1], halo_send.at[1], halo_recv.at[1], me - 1)

    @pl.when(me < wide - 1)
    def _():
        down_copy.start()

    @pl.when(me > 0)
    def _():
        up_copy.start()

    swap = [
        remote(inner_hbm.at[:, :, mate_half], inner.at[core], weight_send.at[0], weight_recv.at[0], mate),
        remote(outer_hbm.at[:, :, mate_half], outer.at[core], weight_send.at[1], weight_recv.at[1], mate),
    ]
    for copy in swap:
        copy.start()

    ext[:, 1 : rows + 1, 8 : 8 + columns, :] = feat[...]
    local[1].wait()
    taps = first.shape[0]
    for t in range(taps):
        high, low = halves(first[t])
        first_hi[t * ch : (t + 1) * ch, :] = high
        first_lo[t * ch : (t + 1) * ch, :] = low
    local[2].wait()
    for t in range(down.shape[0]):
        high, low = halves(down[t])
        down_hi[t * ch : (t + 1) * ch, :] = high
        down_lo[t * ch : (t + 1) * ch, :] = low

    @pl.when(me > 0)
    def _():
        down_copy.wait_recv()
        ext[:, 0, 8 : 8 + columns, :] = halo[0]

    @pl.when(me < wide - 1)
    def _():
        up_copy.wait_recv()
        ext[:, rows + 1, 8 : 8 + columns, :] = halo[1]

    count = fields * rows * columns
    for t in range(taps):
        dr, dc = divmod(t, 3)
        slab = ext[:, dr : dr + rows, 7 + dc : 7 + dc + columns, :].reshape(count, ch)
        high, low = halves(slab)
        cols1[0:count, t * ch : (t + 1) * ch] = high
        cols1[count : 2 * count, t * ch : (t + 1) * ch] = low
    both = dot(cols1[...], first_hi[...])
    activated = both[0:count] + both[count : 2 * count] + dot(cols1[0:count, :], first_lo[...])
    activated = jnp.maximum(activated, 0.0)
    lanes = act.shape[2]
    for piece in range(ch // lanes):
        act[piece] = activated[:, piece * lanes : (piece + 1) * lanes]
    small = fields * out_cols
    for t in range(down.shape[0]):
        dr, dc = divmod(t, 2)
        for piece in range(ch // lanes):
            got = jnp.concatenate(
                [
                    act[piece, pl.ds((f * rows + dr) * columns + dc, out_cols, stride=2), :]
                    for f in range(fields)
                ],
                axis=0,
            )
            high, low = halves(got)
            at = t * ch + piece * lanes
            cols2[0:small, at : at + lanes] = high
            cols2[small : 2 * small, at : at + lanes] = low
    both = dot(cols2[...], down_hi[...])
    reduced = both[0:small] + both[small : 2 * small] + dot(cols2[0:small, :], down_lo[...])
    for c in range(chips):
        red[c] = reduced[:, c * pair : (c + 1) * pair]

    def a2a(k):
        to = lax.rem(me + k, wide)
        return remote(red.at[lax.div(to, 2)], gathered.at[me], a2a_send.at[k], a2a_recv.at[me], to)

    def a2a_start(k, carry):
        a2a(k).start()
        return carry

    lax.fori_loop(1, wide, a2a_start, 0)
    gathered[me] = red[chip]

    local[3].wait()
    swap[0].wait_recv()
    for t in range(taps):
        for q in range(2):
            high, low = halves(inner[q, t])
            at = t * pair + q * own
            for b in range(blocks):
                inner_hi[b, at : at + own, :] = high[:, b * block : (b + 1) * block]
                inner_lo[b, at : at + own, :] = low[:, b * block : (b + 1) * block]

    def a2a_wait(k, carry):
        source = lax.rem(me + k, wide)
        remote(red.at[0], gathered.at[source], a2a_send.at[k], a2a_recv.at[source], source).wait_recv()
        return carry

    lax.fori_loop(1, wide, a2a_wait, 0)

    for f in range(fields):
        ext2[f, 1 : wide + 1, 8 : 8 + out_cols, :] = gathered[:, f * out_cols : (f + 1) * out_cols, :]
    total = fields * field_pos
    for t in range(taps):
        dr, dc = divmod(t, 3)
        slab = ext2[:, dr : dr + wide, 7 + dc : 7 + dc + out_cols, :].reshape(total, pair)
        high, low = halves(slab)
        cols3[0:total, t * pair : (t + 1) * pair] = high
        cols3[total : 2 * total, t * pair : (t + 1) * pair] = low

    my_block = lax.div(chip, per_block)

    def rs(c):
        return remote(part.at[c], scat.at[chip], rs_send.at[c], rs_recv.at[chip], 2 * c + core)

    for step in range(blocks):
        b = lax.rem(my_block + step + 1, blocks)
        both = dot(cols3[...], inner_hi[b])
        value = both[0:total] + both[total : 2 * total] + dot(cols3[0:total, :], inner_lo[b])
        turned = value.T
        for j in range(per_block):
            c = b * per_block + j
            part[c] = turned[j * own : (j + 1) * own]

            @pl.when(c != chip)
            def _():
                rs(c).start()

    local[4].wait()
    swap[1].wait_recv()
    span = taps * pair
    for t in range(taps):
        for q in range(2):
            high, low = halves(outer[q, t])
            at = t * pair + q * own
            for b in range(blocks):
                outer_all[b, at : at + own, :] = high[:, b * block : (b + 1) * block]
                outer_all[b, span + at : span + at + own, :] = low[:, b * block : (b + 1) * block]

    def rs_add(k, value):
        source = lax.rem(chip + k, chips)
        remote(
            part.at[0], scat.at[source], rs_send.at[source], rs_recv.at[source], 2 * source + core
        ).wait_recv()
        return value + scat[source]

    hidden = part[chip]
    for k in range(1, chips):
        hidden = rs_add(k, hidden)
    hid[chip] = jnp.maximum(hidden, 0.0)

    def ag(k):
        to = lax.rem(chip + k, chips)
        return remote(hid.at[chip], hid.at[chip], ag_send.at[k], ag_recv.at[chip], 2 * to + core)

    def ag_start(k, carry):
        ag(k).start()
        return carry

    lax.fori_loop(1, chips, ag_start, 0)

    for step in range(blocks):
        b = lax.rem(my_block + step, blocks)
        for j in range(per_block):
            source = b * per_block + j

            @pl.when(source != chip)
            def _():
                remote(
                    hid.at[chip], hid.at[source], ag_send.at[0], ag_recv.at[source], 2 * source + core
                ).wait_recv()

        high, low = halves(hid[pl.ds(b * per_block, per_block)].reshape(block, total))
        both = dot(outer_all[b], high)
        value = both[0:span] + both[span : 2 * span] + dot(outer_all[b, 0:span, :], low)
        if step == 0:
            taps_out[...] = value
        else:
            taps_out[...] += value

    place = lax.broadcasted_iota(jnp.int32, (own, field_pos), 1)
    row = lax.div(place, out_cols)
    col = lax.rem(place, out_cols)

    def shifted(q, f):
        total_value = jnp.zeros((own, field_pos), F32)
        for t in range(taps):
            dr, dc = divmod(t, 3)
            dr, dc = dr - 1, dc - 1
            at = pl.multiple_of(t * pair + q * own, own)
            value = taps_out[pl.ds(at, own), f * field_pos : (f + 1) * field_pos]
            offset = dr * out_cols + dc
            if offset:
                value = pltpu.roll(value, (-offset) % field_pos, 1)
                good = (row + dr >= 0) & (row + dr < wide) & (col + dc >= 0) & (col + dc < out_cols)
                value = jnp.where(good, value, 0.0)
            total_value = total_value + value
        return total_value

    for f in range(fields):
        mine[:, f * field_pos : (f + 1) * field_pos] = shifted(1 - core, f)
    last = remote(mine, theirs, fin_send.at[0], fin_recv.at[0], mate)
    last.start()
    kept = [shifted(core, f) for f in range(fields)]
    last.wait_recv()
    for f in range(fields):
        value = (kept[f] + theirs[:, f * field_pos : (f + 1) * field_pos]).T
        before = ext2[f, 1 : wide + 1, 8 : 8 + out_cols, :].reshape(field_pos, pair)
        before = jnp.where(core == 0, before[:, 0:own], before[:, own:pair])
        out_ref[f] = jnp.maximum(before + value, 0.0).reshape(wide, out_cols, own)

    @pl.when(me < wide - 1)
    def _():
        down_copy.wait_send()

    @pl.when(me > 0)
    def _():
        up_copy.wait_send()

    for copy in swap:
        copy.wait_send()

    def a2a_done(k, carry):
        a2a(k).wait_send()
        return carry

    lax.fori_loop(1, wide, a2a_done, 0)

    def rs_done(k, carry):
        rs(lax.rem(chip + k, chips)).wait_send()
        ag(k).wait_send()
        return carry

    lax.fori_loop(1, chips, rs_done, 0)
    last.wait_send()


def fused_body(features, first_weight, down_weight, inner_weight, outer_weight):
    wide = lax.axis_size("wide")
    chips = wide // 2
    fields, rows, columns, ch = features.shape
    full = down_weight.shape[3]
    own = full // wide
    pair, half = 2 * own, full // 2
    taps, quads = 9, 4
    out_cols = columns // 2
    total = fields * wide * out_cols
    count, small = fields * rows * columns, fields * out_cols
    block = 256
    blocks = half // block
    first = first_weight.reshape(taps, ch, ch)
    down = down_weight.reshape(quads, ch, full)
    inner = jnp.swapaxes(inner_weight, 3, 4).reshape(taps, own, full)
    outer = jnp.swapaxes(outer_weight, 3, 4).reshape(taps, own, full)
    dma = pltpu.SemaphoreType.DMA
    return pl.pallas_call(
        functools.partial(fused, wide),
        out_shape=jax.ShapeDtypeStruct((fields, wide, out_cols, own), F32),
        in_specs=[pl.BlockSpec(memory_space=pl.ANY)] * 5,
        out_specs=pl.BlockSpec(memory_space=pltpu.VMEM),
        scratch_shapes=[
            pltpu.VMEM(features.shape, F32),
            pltpu.VMEM((taps, ch, ch), F32),
            pltpu.VMEM((quads, ch, full), F32),
            pltpu.VMEM((2, taps, own, half), F32),
            pltpu.VMEM((2, taps, own, half), F32),
            pltpu.VMEM((taps * ch, ch), BF16),
            pltpu.VMEM((taps * ch, ch), BF16),
            pltpu.VMEM((quads * ch, full), BF16),
            pltpu.VMEM((quads * ch, full), BF16),
            pltpu.VMEM((blocks, taps * pair, block), BF16),
            pltpu.VMEM((blocks, taps * pair, block), BF16),
            pltpu.VMEM((blocks, 2 * taps * pair, block), BF16),
            pltpu.VMEM((2, fields, columns, ch), F32),
            pltpu.VMEM((fields, rows + 2, columns + 16, ch), F32),
            pltpu.VMEM((2 * count, taps * ch), BF16),
            pltpu.VMEM((ch // 128, count, 128), F32),
            pltpu.VMEM((2 * small, quads * ch), BF16),
            pltpu.VMEM((chips, small, pair), F32),
            pltpu.VMEM((wide, small, pair), F32),
            pltpu.VMEM((fields, wide + 2, out_cols + 16, pair), F32),
            pltpu.VMEM((2 * total, taps * pair), BF16),
            pltpu.VMEM((chips, own, total), F32),
            pltpu.VMEM((chips, own, total), F32),
            pltpu.VMEM((chips, own, total), F32),
            pltpu.VMEM((taps * pair, total), F32),
            pltpu.VMEM((own, total), F32),
            pltpu.VMEM((own, total), F32),
            dma((5,)), dma((2,)), dma((2,)), dma((2,)), dma((2,)),
            dma((wide,)), dma((wide,)), dma((chips,)), dma((chips,)), dma((chips,)), dma((chips,)),
            dma((1,)), dma((1,)),
        ],
        compiler_params=pltpu.CompilerParams(
            collective_id=0, has_side_effects=True, vmem_limit_bytes=48 << 20
        ),
        cost_estimate=pl.CostEstimate(
            flops=2 * total * taps * full * full // chips, bytes_accessed=12 << 20, transcendentals=0
        ),
    )(features, first, down, inner, outer)


def fits(features, first_weight, down_weight, inner_weight):
    wide = lax.axis_size("wide")
    fields, rows, columns, ch = features.shape
    full = down_weight.shape[3]
    own = full // wide
    return (
        wide % 2 == 0 and rows == 2 and inner_weight.shape[0] == 1 and own % 64 == 0
        and 256 % own == 0 and full % 512 == 0 and ch % 128 == 0 and columns == 16
        and (wide * columns // 2) % 128 == 0 and fields * wide * columns <= 1024
    )


def choose(features, first_weight, down_weight, inner_weight, outer_weight):
    whole = fused_body if fits(features, first_weight, down_weight, inner_weight) else body
    return whole(features, first_weight, down_weight, inner_weight, outer_weight)


def solution(mesh):
    in_specs = (
        P("groups", "wide", None, None),
        P(),
        P(),
        P(None, None, None, None, "wide"),
        P(None, None, None, None, "wide"),
    )
    out_specs = P("groups", None, None, "wide")
    return jax.shard_map(choose, mesh=mesh, in_specs=in_specs, out_specs=out_specs, check_vma=False)
```

```python
import functools

import jax
import jax.numpy as jnp
from jax import lax
from jax.experimental import pallas as pl
from jax.experimental.pallas import tpu as pltpu
from jax.sharding import PartitionSpec as P


def extended_2(shard, sides, width):
    for axis, dim in sides:
        size, length = (lax.axis_size(axis), shard.shape[dim])
        up = [(i, (i + 1) % size) for i in range(size - 1)]
        down = [(j, i) for i, j in up]
        last = lax.slice_in_dim(shard, length - width, length, axis=dim)
        first = lax.slice_in_dim(shard, 0, width, axis=dim)
        before = lax.ppermute(last, axis, up)
        after = lax.ppermute(first, axis, down)
        shard = jnp.concatenate([before, shard, after], axis=dim)
    return shard


def partner_2(block, axis, distance):
    count = lax.axis_size(axis)
    route = []
    for low in range(count):
        high = low | 1 << distance
        if high != low and high < count:
            route += [(low, high), (high, low)]
    return lax.ppermute(block, axis, route)


def convolve(feature_map, kernel, layout, strides, padding):
    return lax.conv_general_dilated(
        feature_map,
        kernel,
        strides,
        padding,
        dimension_numbers=("NHWC", layout, "NHWC"),
        precision=lax.Precision.HIGHEST,
    )


def device_bit(bit_number):
    return lax.axis_index("wide") >> bit_number & 1


def spatial(local_rows, first_weight, down_weight):
    extended = extended_2(local_rows, (("wide", 1),), 1)
    activated = jax.nn.relu(convolve(extended, first_weight, "HWIO", (1, 1), [(0, 0), (1, 1)]))
    return convolve(activated, down_weight, "HWIO", (2, 2), "VALID")


def weight_blocks(stacked, grid_size, low_bits):
    leading = stacked.shape[:-2]
    width = stacked.shape[-2]
    narrow = stacked.shape[-1]
    slots = jnp.moveaxis(stacked.reshape(leading + (grid_size, width // grid_size, narrow)), -3, 0)
    remainder = slots.shape[1:]
    for bit_number in low_bits:
        paired = slots.reshape((grid_size >> bit_number + 1, 2, 1 << bit_number) + remainder)
        lower = paired[:, 0]
        upper = paired[:, 1]
        first_half = device_bit(bit_number) == 0
        outgoing = jnp.where(first_half, upper, lower)
        keeping = jnp.where(first_half, lower, upper)
        incoming = partner_2(outgoing, "wide", bit_number)
        merged = jnp.stack(
            [jnp.where(first_half, keeping, incoming), jnp.where(first_half, incoming, keeping)], 1
        )
        slots = merged.reshape((grid_size,) + remainder)
    joined = jnp.moveaxis(slots, 0, -2)
    return joined.reshape(leading + (width // grid_size, grid_size * narrow))


def channel_pieces(piece, low_bits):
    for bit_number in low_bits:
        partner = partner_2(piece, "wide", bit_number)
        first_half = device_bit(bit_number) == 0
        piece = jnp.where(
            first_half, jnp.concatenate([piece, partner], 3), jnp.concatenate([partner, piece], 3)
        )
    return piece


def group_total(partial_value, bit_list):
    for bit_number in bit_list:
        partial_value = partial_value + partner_2(partial_value, "wide", bit_number)
    return partial_value


def body(features, first_weight, down_weight, inner_weight, outer_weight):
    total_bits = lax.axis_size("wide").bit_length() - 1
    half_bits = total_bits // 2
    grid_size = 1 << half_bits
    low_bits = list(range(half_bits))
    high_bits = list(range(half_bits, total_bits))
    channels = down_weight.shape[3]
    stacked = weight_blocks(jnp.stack([inner_weight, outer_weight], 0), grid_size, low_bits)
    reduced = spatial(features, first_weight, down_weight)
    current = channel_pieces(
        lax.all_to_all(reduced, "wide", split_axis=3, concat_axis=1, tiled=True), low_bits
    )
    kernel_in = stacked[0, 0]
    kernel_out = stacked[1, 0]
    partial_value = convolve(current, kernel_in, "HWOI", (1, 1), "SAME")
    hidden = jax.nn.relu(group_total(partial_value, high_bits))
    partial_value = convolve(hidden, kernel_out, "HWIO", (1, 1), "SAME")
    current = jax.nn.relu(current + group_total(partial_value, low_bits))
    own_count = channels // lax.axis_size("wide")
    offset = lax.axis_index("wide") % grid_size * own_count
    return lax.dynamic_slice_in_dim(current, offset, own_count, 3)

MESH = pl.DeviceIdType.MESH
F32 = jnp.float32
BF16 = jnp.bfloat16


def halves(value):
    high = value.astype(BF16)
    return high, (value - high.astype(F32)).astype(BF16)


def dot(a, b):
    return jnp.dot(a, b, preferred_element_type=F32)


def fused(
    wide,
    feat_hbm, first_hbm, down_hbm, inner_hbm, outer_hbm, out_ref,
    feat, first, down, inner, outer,
    first_hi, first_lo, down_hi, down_lo, inner_hi, inner_lo, outer_all,
    halo, ext, cols1, act, cols2, red, gathered, ext2, cols3,
    part, from_y, to_z, from_z, hid, taps_out, mine, theirs,
    local_sem, halo_send, halo_recv, weight_send, weight_recv,
    a2a_send, a2a_recv, rsy_send, rsy_recv, rsz_send, rsz_recv, agy_send, agz_send, ag_recv,
    fin_send, fin_recv, relay, known,
):
    me = lax.axis_index("wide")
    core = lax.rem(me, 2)
    chip = lax.div(me, 2)
    mate = me + 1 - 2 * core
    chips = wide // 2
    line = chips // 2
    z = lax.div(chip, 2)
    y = lax.rem(chip, 2)
    across = me + 2 - 4 * y
    beside = me - 1 + 2 * core
    fields, rows, columns, ch = feat.shape
    own = inner.shape[2]
    half = inner.shape[3]
    pair = 2 * own
    out_cols = columns // 2
    field_pos = wide * out_cols
    block = inner_hi.shape[2]
    per_block = block // own
    blocks = half // block

    def remote(src, dst, send, recv, device):
        return pltpu.make_async_remote_copy(
            src_ref=src, dst_ref=dst, send_sem=send, recv_sem=recv,
            device_id={"wide": device}, device_id_type=MESH,
        )

    my_half = pl.ds(pl.multiple_of(core * half, half), half)
    mate_half = pl.ds(pl.multiple_of((1 - core) * half, half), half)
    local = [
        pltpu.make_async_copy(feat_hbm, feat, local_sem.at[0]),
        pltpu.make_async_copy(first_hbm, first, local_sem.at[1]),
        pltpu.make_async_copy(down_hbm, down, local_sem.at[2]),
        pltpu.make_async_copy(inner_hbm.at[:, :, my_half], inner.at[core], local_sem.at[3]),
        pltpu.make_async_copy(outer_hbm.at[:, :, my_half], outer.at[core], local_sem.at[4]),
    ]
    for copy in local:
        copy.start()

    barrier = pltpu.get_barrier_semaphore()
    has_below = z > 0
    has_above = z < line - 1
    has_beside = (beside >= 0) & (beside < wide)

    def signal(semaphore, device):
        pl.semaphore_signal(
            semaphore, inc=1, device_id={"wide": device}, device_id_type=MESH
        )

    signal(barrier, mate)
    signal(barrier, across)

    @pl.when(has_beside)
    def _():
        signal(barrier, beside)

    @pl.when(has_below)
    def _():
        signal(barrier, me - 4)

    @pl.when(has_above)
    def _():
        signal(barrier, me + 4)

    def relay_tell(r):
        @pl.when(has_above)
        def _():
            signal(relay.at[2 * r], me + 4)

        @pl.when(has_below)
        def _():
            signal(relay.at[2 * r + 1], me - 4)

    def relay_hear(r):
        @pl.when(has_below)
        def _():
            pl.semaphore_wait(relay.at[2 * r], 1)

        @pl.when(has_above)
        def _():
            pl.semaphore_wait(relay.at[2 * r + 1], 1)

    ext[...] = jnp.zeros_like(ext)
    ext2[...] = jnp.zeros_like(ext2)
    local[0].wait()
    greeted = (
        2 + has_beside.astype(jnp.int32) + has_below.astype(jnp.int32) + has_above.astype(jnp.int32)
    )
    pl.semaphore_wait(barrier, greeted)

    down_copy = remote(feat.at[:, rows - 1], halo.at[0], halo_send.at[0], halo_recv.at[0], me + 1)
    up_copy = remote(feat.at[:, 0], halo.at[1], halo_send.at[1], halo_recv.at[1], me - 1)

    @pl.when(me < wide - 1)
    def _():
        down_copy.start()

    @pl.when(me > 0)
    def _():
        up_copy.start()

    swap = [
        remote(inner_hbm.at[:, :, mate_half], inner.at[core], weight_send.at[0], weight_recv.at[0], mate),
        remote(outer_hbm.at[:, :, mate_half], outer.at[core], weight_send.at[1], weight_recv.at[1], mate),
    ]
    for copy in swap:
        copy.start()

    def prepare_down():
        for t in range(down.shape[0]):
            high, low = halves(down[t])
            down_hi[t * ch : (t + 1) * ch, :] = high
            down_lo[t * ch : (t + 1) * ch, :] = low

    rounds = line - 2
    if rounds:
        relay_tell(0)
    ext[:, 1 : rows + 1, 8 : 8 + columns, :] = feat[...]
    local[1].wait()
    taps = first.shape[0]
    for t in range(taps):
        high, low = halves(first[t])
        first_hi[t * ch : (t + 1) * ch, :] = high
        first_lo[t * ch : (t + 1) * ch, :] = low
    for r in range(rounds):
        relay_hear(r)
        if r + 1 < rounds:
            relay_tell(r + 1)
        if r == 0:
            local[2].wait()
            prepare_down()
    if not rounds:
        local[2].wait()
        prepare_down()
    signal(known.at[0], across)

    @pl.when(me > 0)
    def _():
        down_copy.wait_recv()
        ext[:, 0, 8 : 8 + columns, :] = halo[0]

    @pl.when(me < wide - 1)
    def _():
        up_copy.wait_recv()
        ext[:, rows + 1, 8 : 8 + columns, :] = halo[1]

    pl.semaphore_wait(known.at[0], 1)
    signal(known.at[1], mate)
    count = fields * rows * columns
    for t in range(taps):
        dr, dc = divmod(t, 3)
        slab = ext[:, dr : dr + rows, 7 + dc : 7 + dc + columns, :].reshape(count, ch)
        high, low = halves(slab)
        cols1[0:count, t * ch : (t + 1) * ch] = high
        cols1[count : 2 * count, t * ch : (t + 1) * ch] = low
    both = dot(cols1[...], first_hi[...])
    activated = both[0:count] + both[count : 2 * count] + dot(cols1[0:count, :], first_lo[...])
    activated = jnp.maximum(activated, 0.0)
    lanes = act.shape[2]
    for piece in range(ch // lanes):
        act[piece] = activated[:, piece * lanes : (piece + 1) * lanes]
    small = fields * out_cols
    for t in range(down.shape[0]):
        dr, dc = divmod(t, 2)
        for piece in range(ch // lanes):
            got = jnp.concatenate(
                [
                    act[piece, pl.ds((f * rows + dr) * columns + dc, out_cols, stride=2), :]
                    for f in range(fields)
                ],
                axis=0,
            )
            high, low = halves(got)
            at = t * ch + piece * lanes
            cols2[0:small, at : at + lanes] = high
            cols2[small : 2 * small, at : at + lanes] = low
    both = dot(cols2[...], down_hi[...])
    reduced = both[0:small] + both[small : 2 * small] + dot(cols2[0:small, :], down_lo[...])
    for c in range(chips):
        red[c] = reduced[:, c * pair : (c + 1) * pair]

    def a2a(k):
        to = lax.rem(me + k, wide)
        return remote(red.at[lax.div(to, 2)], gathered.at[me], a2a_send.at[k], a2a_recv.at[me], to)

    def a2a_start(k, carry):
        a2a(k).start()
        return carry

    pl.semaphore_wait(known.at[1], 1)
    lax.fori_loop(1, wide, a2a_start, 0)
    gathered[me] = red[chip]

    local[3].wait()
    swap[0].wait_recv()
    for t in range(taps):
        for q in range(2):
            high, low = halves(inner[q, t])
            at = t * pair + q * own
            for b in range(blocks):
                inner_hi[b, at : at + own, :] = high[:, b * block : (b + 1) * block]
                inner_lo[b, at : at + own, :] = low[:, b * block : (b + 1) * block]

    def a2a_wait(k, carry):
        source = lax.rem(me + k, wide)
        remote(red.at[0], gathered.at[source], a2a_send.at[k], a2a_recv.at[source], source).wait_recv()
        return carry

    lax.fori_loop(1, wide, a2a_wait, 0)

    for f in range(fields):
        ext2[f, 1 : wide + 1, 8 : 8 + out_cols, :] = gathered[:, f * out_cols : (f + 1) * out_cols, :]
    total = fields * field_pos
    for t in range(taps):
        dr, dc = divmod(t, 3)
        slab = ext2[:, dr : dr + wide, 7 + dc : 7 + dc + out_cols, :].reshape(total, pair)
        high, low = halves(slab)
        cols3[0:total, t * pair : (t + 1) * pair] = high
        cols3[total : 2 * total, t * pair : (t + 1) * pair] = low

    my_block = lax.div(chip, per_block)

    half_block = per_block // 2

    def rs_y(zz):
        return remote(
            part.at[2 * zz + 1 - y], from_y.at[zz], rsy_send.at[zz], rsy_recv.at[zz], across
        )

    def rs_z(zz):
        return remote(
            to_z.at[zz], from_z.at[z], rsz_send.at[zz], rsz_recv.at[z], 4 * zz + 2 * y + core
        )

    for step in range(blocks):
        b = lax.rem(my_block + step + 1, blocks)
        both = dot(cols3[...], inner_hi[b])
        value = both[0:total] + both[total : 2 * total] + dot(cols3[0:total, :], inner_lo[b])
        turned = value.T
        for j in range(per_block):
            part[b * per_block + j] = turned[j * own : (j + 1) * own]
        for j in range(half_block):
            rs_y(b * half_block + j).start()

    for step in range(blocks):
        b = lax.rem(my_block + step + 1, blocks)
        for j in range(half_block):
            zz = b * half_block + j
            rs_y(zz).wait_recv()
            to_z[zz] = part[2 * zz + y] + from_y[zz]

            @pl.when(zz != z)
            def _():
                rs_z(zz).start()

    local[4].wait()
    swap[1].wait_recv()
    span = taps * pair
    for t in range(taps):
        for q in range(2):
            high, low = halves(outer[q, t])
            at = t * pair + q * own
            for b in range(blocks):
                outer_all[b, at : at + own, :] = high[:, b * block : (b + 1) * block]
                outer_all[b, span + at : span + at + own, :] = low[:, b * block : (b + 1) * block]

    hidden = to_z[z]
    for k in range(1, line):
        source = lax.rem(z + k, line)
        remote(
            to_z.at[0], from_z.at[source], rsz_send.at[source], rsz_recv.at[source],
            4 * source + 2 * y + core,
        ).wait_recv()
        hidden = hidden + from_z[source]
    hid[chip] = jnp.maximum(hidden, 0.0)

    def ag_z(zz):
        return remote(
            hid.at[chip], hid.at[chip], agz_send.at[zz], ag_recv.at[chip], 4 * zz + 2 * y + core
        )

    def ag_y(zz):
        c = 2 * zz + y
        return remote(hid.at[c], hid.at[c], agy_send.at[zz], ag_recv.at[c], across)

    def arrived(c, device):
        remote(hid.at[chip], hid.at[c], agz_send.at[0], ag_recv.at[c], device).wait_recv()

    for step in range(blocks):
        b = lax.rem(my_block + step + 1, blocks)
        for j in range(half_block):
            zz = b * half_block + j

            @pl.when(zz != z)
            def _():
                ag_z(zz).start()

    ag_y(z).start()
    for step in range(blocks):
        b = lax.rem(my_block + step, blocks)
        for j in range(half_block):
            zz = b * half_block + j

            @pl.when(zz != z)
            def _():
                arrived(2 * zz + y, 4 * zz + 2 * y + core)
                ag_y(zz).start()

        for j in range(half_block):
            arrived(2 * (b * half_block + j) + 1 - y, across)

        high, low = halves(hid[pl.ds(b * per_block, per_block)].reshape(block, total))
        both = dot(outer_all[b], high)
        value = both[0:span] + both[span : 2 * span] + dot(outer_all[b, 0:span, :], low)
        if step == 0:
            taps_out[...] = value
        else:
            taps_out[...] += value

    place = lax.broadcasted_iota(jnp.int32, (own, field_pos), 1)
    row = lax.div(place, out_cols)
    col = lax.rem(place, out_cols)

    def shifted(q, f):
        total_value = jnp.zeros((own, field_pos), F32)
        for t in range(taps):
            dr, dc = divmod(t, 3)
            dr, dc = dr - 1, dc - 1
            at = pl.multiple_of(t * pair + q * own, own)
            value = taps_out[pl.ds(at, own), f * field_pos : (f + 1) * field_pos]
            offset = dr * out_cols + dc
            if offset:
                value = pltpu.roll(value, (-offset) % field_pos, 1)
                good = (row + dr >= 0) & (row + dr < wide) & (col + dc >= 0) & (col + dc < out_cols)
                value = jnp.where(good, value, 0.0)
            total_value = total_value + value
        return total_value

    for f in range(fields):
        mine[:, f * field_pos : (f + 1) * field_pos] = shifted(1 - core, f)
    last = remote(mine, theirs, fin_send.at[0], fin_recv.at[0], mate)
    last.start()
    kept = [shifted(core, f) for f in range(fields)]
    last.wait_recv()
    for f in range(fields):
        value = (kept[f] + theirs[:, f * field_pos : (f + 1) * field_pos]).T
        before = ext2[f, 1 : wide + 1, 8 : 8 + out_cols, :].reshape(field_pos, pair)
        before = jnp.where(core == 0, before[:, 0:own], before[:, own:pair])
        out_ref[f] = jnp.maximum(before + value, 0.0).reshape(wide, out_cols, own)

    @pl.when(me < wide - 1)
    def _():
        down_copy.wait_send()

    @pl.when(me > 0)
    def _():
        up_copy.wait_send()

    for copy in swap:
        copy.wait_send()

    def a2a_done(k, carry):
        a2a(k).wait_send()
        return carry

    lax.fori_loop(1, wide, a2a_done, 0)

    for zz in range(line):
        rs_y(zz).wait_send()
        ag_y(zz).wait_send()

        @pl.when(zz != z)
        def _():
            rs_z(zz).wait_send()
            ag_z(zz).wait_send()

    last.wait_send()


def fused_body(features, first_weight, down_weight, inner_weight, outer_weight):
    wide = lax.axis_size("wide")
    chips = wide // 2
    fields, rows, columns, ch = features.shape
    full = down_weight.shape[3]
    own = full // wide
    pair, half = 2 * own, full // 2
    taps, quads = 9, 4
    out_cols = columns // 2
    total = fields * wide * out_cols
    count, small = fields * rows * columns, fields * out_cols
    block = 256
    blocks = half // block
    first = first_weight.reshape(taps, ch, ch)
    down = down_weight.reshape(quads, ch, full)
    inner = jnp.swapaxes(inner_weight, 3, 4).reshape(taps, own, full)
    outer = jnp.swapaxes(outer_weight, 3, 4).reshape(taps, own, full)
    dma = pltpu.SemaphoreType.DMA
    return pl.pallas_call(
        functools.partial(fused, wide),
        out_shape=jax.ShapeDtypeStruct((fields, wide, out_cols, own), F32),
        in_specs=[pl.BlockSpec(memory_space=pl.ANY)] * 5,
        out_specs=pl.BlockSpec(memory_space=pltpu.VMEM),
        scratch_shapes=[
            pltpu.VMEM(features.shape, F32),
            pltpu.VMEM((taps, ch, ch), F32),
            pltpu.VMEM((quads, ch, full), F32),
            pltpu.VMEM((2, taps, own, half), F32),
            pltpu.VMEM((2, taps, own, half), F32),
            pltpu.VMEM((taps * ch, ch), BF16),
            pltpu.VMEM((taps * ch, ch), BF16),
            pltpu.VMEM((quads * ch, full), BF16),
            pltpu.VMEM((quads * ch, full), BF16),
            pltpu.VMEM((blocks, taps * pair, block), BF16),
            pltpu.VMEM((blocks, taps * pair, block), BF16),
            pltpu.VMEM((blocks, 2 * taps * pair, block), BF16),
            pltpu.VMEM((2, fields, columns, ch), F32),
            pltpu.VMEM((fields, rows + 2, columns + 16, ch), F32),
            pltpu.VMEM((2 * count, taps * ch), BF16),
            pltpu.VMEM((ch // 128, count, 128), F32),
            pltpu.VMEM((2 * small, quads * ch), BF16),
            pltpu.VMEM((chips, small, pair), F32),
            pltpu.VMEM((wide, small, pair), F32),
            pltpu.VMEM((fields, wide + 2, out_cols + 16, pair), F32),
            pltpu.VMEM((2 * total, taps * pair), BF16),
            pltpu.VMEM((chips, own, total), F32),
            pltpu.VMEM((chips // 2, own, total), F32),
            pltpu.VMEM((chips // 2, own, total), F32),
            pltpu.VMEM((chips // 2, own, total), F32),
            pltpu.VMEM((chips, own, total), F32),
            pltpu.VMEM((taps * pair, total), F32),
            pltpu.VMEM((own, total), F32),
            pltpu.VMEM((own, total), F32),
            dma((5,)), dma((2,)), dma((2,)), dma((2,)), dma((2,)),
            dma((wide,)), dma((wide,)), dma((chips // 2,)), dma((chips // 2,)), dma((chips // 2,)),
            dma((chips // 2,)), dma((chips // 2,)), dma((chips // 2,)), dma((chips,)),
            dma((1,)), dma((1,)),
            pltpu.SemaphoreType.REGULAR((max(2, chips - 4),)), pltpu.SemaphoreType.REGULAR((2,)),
        ],
        compiler_params=pltpu.CompilerParams(
            collective_id=0, has_side_effects=True, vmem_limit_bytes=62 << 20
        ),
        cost_estimate=pl.CostEstimate(
            flops=2 * total * taps * full * full // chips, bytes_accessed=12 << 20, transcendentals=0
        ),
    )(features, first, down, inner, outer)


def fits(features, first_weight, down_weight, inner_weight):
    wide = lax.axis_size("wide")
    fields, rows, columns, ch = features.shape
    full = down_weight.shape[3]
    own = full // wide
    return (
        wide % 8 == 0 and rows == 2 and inner_weight.shape[0] == 1 and own % 64 == 0
        and 128 % own == 0 and full % 512 == 0 and ch % 128 == 0 and columns == 16
        and (wide * columns // 2) % 128 == 0 and fields * wide * columns <= 1024
    )


def choose(features, first_weight, down_weight, inner_weight, outer_weight):
    whole = fused_body if fits(features, first_weight, down_weight, inner_weight) else body
    return whole(features, first_weight, down_weight, inner_weight, outer_weight)


def solution(mesh):
    in_specs = (
        P("groups", "wide", None, None),
        P(),
        P(),
        P(None, None, None, None, "wide"),
        P(None, None, None, None, "wide"),
    )
    out_specs = P("groups", None, None, "wide")
    return jax.shard_map(choose, mesh=mesh, in_specs=in_specs, out_specs=out_specs, check_vma=False)
```

```python
import functools

import jax
import jax.numpy as jnp
from jax import lax
from jax.experimental import pallas as pl
from jax.experimental.pallas import tpu as pltpu
from jax.sharding import PartitionSpec as P


def extended_2(shard, sides, width):
    for axis, dim in sides:
        size, length = (lax.axis_size(axis), shard.shape[dim])
        up = [(i, (i + 1) % size) for i in range(size - 1)]
        down = [(j, i) for i, j in up]
        last = lax.slice_in_dim(shard, length - width, length, axis=dim)
        first = lax.slice_in_dim(shard, 0, width, axis=dim)
        before = lax.ppermute(last, axis, up)
        after = lax.ppermute(first, axis, down)
        shard = jnp.concatenate([before, shard, after], axis=dim)
    return shard


def partner_2(block, axis, distance):
    count = lax.axis_size(axis)
    route = []
    for low in range(count):
        high = low | 1 << distance
        if high != low and high < count:
            route += [(low, high), (high, low)]
    return lax.ppermute(block, axis, route)


def convolve(feature_map, kernel, layout, strides, padding):
    return lax.conv_general_dilated(
        feature_map,
        kernel,
        strides,
        padding,
        dimension_numbers=("NHWC", layout, "NHWC"),
        precision=lax.Precision.HIGHEST,
    )


def device_bit(bit_number):
    return lax.axis_index("wide") >> bit_number & 1


def spatial(local_rows, first_weight, down_weight):
    extended = extended_2(local_rows, (("wide", 1),), 1)
    activated = jax.nn.relu(convolve(extended, first_weight, "HWIO", (1, 1), [(0, 0), (1, 1)]))
    return convolve(activated, down_weight, "HWIO", (2, 2), "VALID")


def weight_blocks(stacked, grid_size, low_bits):
    leading = stacked.shape[:-2]
    width = stacked.shape[-2]
    narrow = stacked.shape[-1]
    slots = jnp.moveaxis(stacked.reshape(leading + (grid_size, width // grid_size, narrow)), -3, 0)
    remainder = slots.shape[1:]
    for bit_number in low_bits:
        paired = slots.reshape((grid_size >> bit_number + 1, 2, 1 << bit_number) + remainder)
        lower = paired[:, 0]
        upper = paired[:, 1]
        first_half = device_bit(bit_number) == 0
        outgoing = jnp.where(first_half, upper, lower)
        keeping = jnp.where(first_half, lower, upper)
        incoming = partner_2(outgoing, "wide", bit_number)
        merged = jnp.stack(
            [jnp.where(first_half, keeping, incoming), jnp.where(first_half, incoming, keeping)], 1
        )
        slots = merged.reshape((grid_size,) + remainder)
    joined = jnp.moveaxis(slots, 0, -2)
    return joined.reshape(leading + (width // grid_size, grid_size * narrow))


def channel_pieces(piece, low_bits):
    for bit_number in low_bits:
        partner = partner_2(piece, "wide", bit_number)
        first_half = device_bit(bit_number) == 0
        piece = jnp.where(
            first_half, jnp.concatenate([piece, partner], 3), jnp.concatenate([partner, piece], 3)
        )
    return piece


def group_total(partial_value, bit_list):
    for bit_number in bit_list:
        partial_value = partial_value + partner_2(partial_value, "wide", bit_number)
    return partial_value


def body(features, first_weight, down_weight, inner_weight, outer_weight):
    total_bits = lax.axis_size("wide").bit_length() - 1
    half_bits = total_bits // 2
    grid_size = 1 << half_bits
    low_bits = list(range(half_bits))
    high_bits = list(range(half_bits, total_bits))
    channels = down_weight.shape[3]
    stacked = weight_blocks(jnp.stack([inner_weight, outer_weight], 0), grid_size, low_bits)
    reduced = spatial(features, first_weight, down_weight)
    current = channel_pieces(
        lax.all_to_all(reduced, "wide", split_axis=3, concat_axis=1, tiled=True), low_bits
    )
    kernel_in = stacked[0, 0]
    kernel_out = stacked[1, 0]
    partial_value = convolve(current, kernel_in, "HWOI", (1, 1), "SAME")
    hidden = jax.nn.relu(group_total(partial_value, high_bits))
    partial_value = convolve(hidden, kernel_out, "HWIO", (1, 1), "SAME")
    current = jax.nn.relu(current + group_total(partial_value, low_bits))
    own_count = channels // lax.axis_size("wide")
    offset = lax.axis_index("wide") % grid_size * own_count
    return lax.dynamic_slice_in_dim(current, offset, own_count, 3)

MESH = pl.DeviceIdType.MESH
F32 = jnp.float32
BF16 = jnp.bfloat16


def halves(value):
    high = value.astype(BF16)
    return high, (value - high.astype(F32)).astype(BF16)


def dot(a, b):
    return jnp.dot(a, b, preferred_element_type=F32)


def fused(
    wide,
    feat_hbm, first_hbm, down_hbm, inner_hbm, outer_hbm, out_ref,
    feat, first, down, inner, outer,
    first_hi, first_lo, down_hi, down_lo, inner_hi, inner_lo, outer_all,
    halo, ext, cols1, act, cols2, red, gathered, ext2, cols3,
    part, from_y, to_z, from_z, hid, taps_out, mine, theirs,
    local_sem, halo_send, halo_recv, weight_send, weight_recv,
    a2a_send, a2a_recv, rsy_send, rsy_recv, rsz_send, rsz_recv, agy_send, agz_send, ag_recv,
    fin_send, fin_recv, relay, known,
):
    me = lax.axis_index("wide")
    core = lax.rem(me, 2)
    chip = lax.div(me, 2)
    mate = me + 1 - 2 * core
    chips = wide // 2
    line = chips // 2
    z = lax.div(chip, 2)
    y = lax.rem(chip, 2)
    across = me + 2 - 4 * y
    beside = me - 1 + 2 * core
    fields, rows, columns, ch = feat.shape
    own = inner.shape[2]
    half = inner.shape[3]
    pair = 2 * own
    out_cols = columns // 2
    field_pos = wide * out_cols
    block = inner_hi.shape[2]
    per_block = block // own
    blocks = half // block

    def remote(src, dst, send, recv, device):
        return pltpu.make_async_remote_copy(
            src_ref=src, dst_ref=dst, send_sem=send, recv_sem=recv,
            device_id={"wide": device}, device_id_type=MESH,
        )

    my_half = pl.ds(pl.multiple_of(core * half, half), half)
    mate_half = pl.ds(pl.multiple_of((1 - core) * half, half), half)
    local = [
        pltpu.make_async_copy(feat_hbm, feat, local_sem.at[0]),
        pltpu.make_async_copy(first_hbm, first, local_sem.at[1]),
        pltpu.make_async_copy(down_hbm, down, local_sem.at[2]),
        pltpu.make_async_copy(inner_hbm.at[:, :, my_half], inner.at[core], local_sem.at[3]),
        pltpu.make_async_copy(outer_hbm.at[:, :, my_half], outer.at[core], local_sem.at[4]),
    ]
    for copy in local:
        copy.start()

    barrier = pltpu.get_barrier_semaphore()
    has_below = z > 0
    has_above = z < line - 1
    has_beside = (beside >= 0) & (beside < wide)

    def signal(semaphore, device):
        pl.semaphore_signal(
            semaphore, inc=1, device_id={"wide": device}, device_id_type=MESH
        )

    signal(barrier, mate)
    signal(barrier, across)

    @pl.when(has_beside)
    def _():
        signal(barrier, beside)

    @pl.when(has_below)
    def _():
        signal(barrier, me - 4)

    @pl.when(has_above)
    def _():
        signal(barrier, me + 4)

    def relay_tell(r):
        @pl.when(has_above)
        def _():
            signal(relay.at[2 * r], me + 4)

        @pl.when(has_below)
        def _():
            signal(relay.at[2 * r + 1], me - 4)

    def relay_hear(r):
        @pl.when(has_below)
        def _():
            pl.semaphore_wait(relay.at[2 * r], 1)

        @pl.when(has_above)
        def _():
            pl.semaphore_wait(relay.at[2 * r + 1], 1)

    ext[...] = jnp.zeros_like(ext)
    ext2[...] = jnp.zeros_like(ext2)
    local[0].wait()
    greeted = (
        2 + has_beside.astype(jnp.int32) + has_below.astype(jnp.int32) + has_above.astype(jnp.int32)
    )
    pl.semaphore_wait(barrier, greeted)

    down_copy = remote(feat.at[:, rows - 1], halo.at[0], halo_send.at[0], halo_recv.at[0], me + 1)
    up_copy = remote(feat.at[:, 0], halo.at[1], halo_send.at[1], halo_recv.at[1], me - 1)

    @pl.when(me < wide - 1)
    def _():
        down_copy.start()

    @pl.when(me > 0)
    def _():
        up_copy.start()

    swap = [
        remote(inner_hbm.at[:, :, mate_half], inner.at[core], weight_send.at[0], weight_recv.at[0], mate),
        remote(outer_hbm.at[:, :, mate_half], outer.at[core], weight_send.at[1], weight_recv.at[1], mate),
    ]
    for copy in swap:
        copy.start()

    def prepare_down():
        for t in range(down.shape[0]):
            high, low = halves(down[t])
            down_hi[t * ch : (t + 1) * ch, :] = high
            down_lo[t * ch : (t + 1) * ch, :] = low

    rounds = line - 2
    if rounds:
        relay_tell(0)
    ext[:, 1 : rows + 1, 8 : 8 + columns, :] = feat[...]
    local[1].wait()
    taps = first.shape[0]
    for t in range(taps):
        high, low = halves(first[t])
        first_hi[t * ch : (t + 1) * ch, :] = high
        first_lo[t * ch : (t + 1) * ch, :] = low
    for r in range(rounds):
        relay_hear(r)
        if r + 1 < rounds:
            relay_tell(r + 1)
        if r == 0:
            local[2].wait()
            prepare_down()
    if not rounds:
        local[2].wait()
        prepare_down()
    signal(known.at[0], across)

    @pl.when(me > 0)
    def _():
        down_copy.wait_recv()
        ext[:, 0, 8 : 8 + columns, :] = halo[0]

    @pl.when(me < wide - 1)
    def _():
        up_copy.wait_recv()
        ext[:, rows + 1, 8 : 8 + columns, :] = halo[1]

    pl.semaphore_wait(known.at[0], 1)
    signal(known.at[1], mate)
    count = fields * rows * columns
    for t in range(taps):
        dr, dc = divmod(t, 3)
        slab = ext[:, dr : dr + rows, 7 + dc : 7 + dc + columns, :].reshape(count, ch)
        high, low = halves(slab)
        cols1[0:count, t * ch : (t + 1) * ch] = high
        cols1[count : 2 * count, t * ch : (t + 1) * ch] = low
    both = dot(cols1[...], first_hi[...])
    activated = both[0:count] + both[count : 2 * count] + dot(cols1[0:count, :], first_lo[...])
    activated = jnp.maximum(activated, 0.0)
    lanes = act.shape[2]
    for piece in range(ch // lanes):
        act[piece] = activated[:, piece * lanes : (piece + 1) * lanes]
    small = fields * out_cols
    for t in range(down.shape[0]):
        dr, dc = divmod(t, 2)
        for piece in range(ch // lanes):
            got = jnp.concatenate(
                [
                    act[piece, pl.ds((f * rows + dr) * columns + dc, out_cols, stride=2), :]
                    for f in range(fields)
                ],
                axis=0,
            )
            high, low = halves(got)
            at = t * ch + piece * lanes
            cols2[0:small, at : at + lanes] = high
            cols2[small : 2 * small, at : at + lanes] = low
    both = dot(cols2[...], down_hi[...])
    reduced = both[0:small] + both[small : 2 * small] + dot(cols2[0:small, :], down_lo[...])
    for c in range(chips):
        red[c] = reduced[:, c * pair : (c + 1) * pair]

    def a2a(k):
        to = lax.rem(me + k, wide)
        return remote(red.at[lax.div(to, 2)], gathered.at[me], a2a_send.at[k], a2a_recv.at[me], to)

    def a2a_start(k, carry):
        a2a(k).start()
        return carry

    pl.semaphore_wait(known.at[1], 1)
    lax.fori_loop(1, wide, a2a_start, 0)
    gathered[me] = red[chip]

    local[3].wait()
    swap[0].wait_recv()
    for t in range(taps):
        for q in range(2):
            high, low = halves(inner[q, t])
            at = t * pair + q * own
            for b in range(blocks):
                inner_hi[b, at : at + own, :] = high[:, b * block : (b + 1) * block]
                inner_lo[b, at : at + own, :] = low[:, b * block : (b + 1) * block]

    def a2a_wait(k, carry):
        source = lax.rem(me + k, wide)
        remote(red.at[0], gathered.at[source], a2a_send.at[k], a2a_recv.at[source], source).wait_recv()
        return carry

    lax.fori_loop(1, wide, a2a_wait, 0)

    for f in range(fields):
        ext2[f, 1 : wide + 1, 8 : 8 + out_cols, :] = gathered[:, f * out_cols : (f + 1) * out_cols, :]
    my_block = lax.div(chip, per_block)
    half_block = per_block // 2

    def rs_y(f, zz):
        at = f * line + zz
        return remote(
            part.at[f * chips + 2 * zz + 1 - y], from_y.at[at], rsy_send.at[at], rsy_recv.at[at], across
        )

    def rs_z(f, zz):
        at = f * line
        return remote(
            to_z.at[at + zz], from_z.at[at + z], rsz_send.at[at + zz], rsz_recv.at[at + z],
            4 * zz + 2 * y + core,
        )

    for f in range(fields):
        for t in range(taps):
            dr, dc = divmod(t, 3)
            slab = ext2[f, dr : dr + wide, 7 + dc : 7 + dc + out_cols, :].reshape(field_pos, pair)
            high, low = halves(slab)
            cols3[f, 0:field_pos, t * pair : (t + 1) * pair] = high
            cols3[f, field_pos : 2 * field_pos, t * pair : (t + 1) * pair] = low
        for step in range(blocks):
            b = lax.rem(my_block + step + 1, blocks)
            both = dot(cols3[f], inner_hi[b])
            value = both[0:field_pos] + both[field_pos:] + dot(cols3[f, 0:field_pos, :], inner_lo[b])
            turned = value.T
            for j in range(per_block):
                part[f * chips + b * per_block + j] = turned[j * own : (j + 1) * own]
            for j in range(half_block):
                rs_y(f, b * half_block + j).start()

    def pass_on(f):
        for step in range(blocks):
            b = lax.rem(my_block + step + 1, blocks)
            for j in range(half_block):
                zz = b * half_block + j
                rs_y(f, zz).wait_recv()
                to_z[f * line + zz] = part[f * chips + 2 * zz + y] + from_y[f * line + zz]

                @pl.when(zz != z)
                def _():
                    rs_z(f, zz).start()

    local[4].wait()
    swap[1].wait_recv()
    span = taps * pair
    for t in range(taps):
        for q in range(2):
            high, low = halves(outer[q, t])
            at = t * pair + q * own
            for b in range(blocks):
                outer_all[b, at : at + own, :] = high[:, b * block : (b + 1) * block]
                outer_all[b, span + at : span + at + own, :] = low[:, b * block : (b + 1) * block]

    for f in range(fields):
        pass_on(f)

    def ag_z(f, zz):
        at = f * chips + chip
        return remote(
            hid.at[at], hid.at[at], agz_send.at[f * line + zz], ag_recv.at[at], 4 * zz + 2 * y + core
        )

    def ag_y(f, zz):
        at = f * chips + 2 * zz + y
        return remote(hid.at[at], hid.at[at], agy_send.at[f * line + zz], ag_recv.at[at], across)

    def arrived(f, c, device):
        at = f * chips + c
        remote(hid.at[at], hid.at[at], agz_send.at[0], ag_recv.at[at], device).wait_recv()

    def collect(f):
        hidden = to_z[f * line + z]
        for k in range(1, line):
            source = lax.rem(z + k, line)
            at = f * line + source
            remote(
                to_z.at[0], from_z.at[at], rsz_send.at[at], rsz_recv.at[at], 4 * source + 2 * y + core
            ).wait_recv()
            hidden = hidden + from_z[at]
        hid[f * chips + chip] = jnp.maximum(hidden, 0.0)
        for step in range(blocks):
            b = lax.rem(my_block + step + 1, blocks)
            for j in range(half_block):
                zz = b * half_block + j

                @pl.when(zz != z)
                def _():
                    ag_z(f, zz).start()

        ag_y(f, z).start()

    def forward(f, step):
        b = lax.rem(my_block + step, blocks)
        for j in range(half_block):
            zz = b * half_block + j

            @pl.when(zz != z)
            def _():
                arrived(f, 2 * zz + y, 4 * zz + 2 * y + core)
                ag_y(f, zz).start()

    def multiply(f, step):
        b = lax.rem(my_block + step, blocks)
        for j in range(half_block):
            arrived(f, 2 * (b * half_block + j) + 1 - y, across)
        gained = hid[pl.ds(f * chips + b * per_block, per_block)].reshape(block, field_pos)
        high, low = halves(gained)
        both = dot(outer_all[b], high)
        value = both[0:span] + both[span : 2 * span] + dot(outer_all[b, 0:span, :], low)
        if step == 0:
            taps_out[f] = value
        else:
            taps_out[f] += value

    place = lax.broadcasted_iota(jnp.int32, (own, field_pos), 1)
    row = lax.div(place, out_cols)
    col = lax.rem(place, out_cols)

    def shifted(q, f):
        total_value = jnp.zeros((own, field_pos), F32)
        for t in range(taps):
            dr, dc = divmod(t, 3)
            dr, dc = dr - 1, dc - 1
            at = pl.multiple_of(t * pair + q * own, own)
            value = taps_out[f, pl.ds(at, own), :]
            offset = dr * out_cols + dc
            if offset:
                value = pltpu.roll(value, (-offset) % field_pos, 1)
                good = (row + dr >= 0) & (row + dr < wide) & (col + dc >= 0) & (col + dc < out_cols)
                value = jnp.where(good, value, 0.0)
            total_value = total_value + value
        return total_value

    def last(f):
        return remote(mine.at[f], theirs.at[f], fin_send.at[f], fin_recv.at[f], mate)

    def give(f):
        mine[f] = shifted(1 - core, f)
        last(f).start()

    for f in range(fields):
        collect(f)
    for step in range(blocks):
        forward(0, step)
    for f in range(fields):
        for step in range(blocks):
            multiply(f, step)
            if f + 1 < fields:
                forward(f + 1, step)
        give(f)
    for f in range(fields):
        kept = shifted(core, f)
        last(f).wait_recv()
        value = (kept + theirs[f]).T
        before = ext2[f, 1 : wide + 1, 8 : 8 + out_cols, :].reshape(field_pos, pair)
        before = jnp.where(core == 0, before[:, 0:own], before[:, own:pair])
        out_ref[f] = jnp.maximum(before + value, 0.0).reshape(wide, out_cols, own)

    @pl.when(me < wide - 1)
    def _():
        down_copy.wait_send()

    @pl.when(me > 0)
    def _():
        up_copy.wait_send()

    for copy in swap:
        copy.wait_send()

    def a2a_done(k, carry):
        a2a(k).wait_send()
        return carry

    lax.fori_loop(1, wide, a2a_done, 0)

    for f in range(fields):
        last(f).wait_send()
        for zz in range(line):
            rs_y(f, zz).wait_send()
            ag_y(f, zz).wait_send()

            @pl.when(zz != z)
            def _():
                rs_z(f, zz).wait_send()
                ag_z(f, zz).wait_send()


def fused_body(features, first_weight, down_weight, inner_weight, outer_weight):
    wide = lax.axis_size("wide")
    chips = wide // 2
    fields, rows, columns, ch = features.shape
    full = down_weight.shape[3]
    own = full // wide
    pair, half = 2 * own, full // 2
    taps, quads = 9, 4
    out_cols = columns // 2
    place, line = wide * out_cols, chips // 2
    total = fields * place
    count, small = fields * rows * columns, fields * out_cols
    block = 256
    blocks = half // block
    first = first_weight.reshape(taps, ch, ch)
    down = down_weight.reshape(quads, ch, full)
    inner = jnp.swapaxes(inner_weight, 3, 4).reshape(taps, own, full)
    outer = jnp.swapaxes(outer_weight, 3, 4).reshape(taps, own, full)
    dma = pltpu.SemaphoreType.DMA
    return pl.pallas_call(
        functools.partial(fused, wide),
        out_shape=jax.ShapeDtypeStruct((fields, wide, out_cols, own), F32),
        in_specs=[pl.BlockSpec(memory_space=pl.ANY)] * 5,
        out_specs=pl.BlockSpec(memory_space=pltpu.VMEM),
        scratch_shapes=[
            pltpu.VMEM(features.shape, F32),
            pltpu.VMEM((taps, ch, ch), F32),
            pltpu.VMEM((quads, ch, full), F32),
            pltpu.VMEM((2, taps, own, half), F32),
            pltpu.VMEM((2, taps, own, half), F32),
            pltpu.VMEM((taps * ch, ch), BF16),
            pltpu.VMEM((taps * ch, ch), BF16),
            pltpu.VMEM((quads * ch, full), BF16),
            pltpu.VMEM((quads * ch, full), BF16),
            pltpu.VMEM((blocks, taps * pair, block), BF16),
            pltpu.VMEM((blocks, taps * pair, block), BF16),
            pltpu.VMEM((blocks, 2 * taps * pair, block), BF16),
            pltpu.VMEM((2, fields, columns, ch), F32),
            pltpu.VMEM((fields, rows + 2, columns + 16, ch), F32),
            pltpu.VMEM((2 * count, taps * ch), BF16),
            pltpu.VMEM((ch // 128, count, 128), F32),
            pltpu.VMEM((2 * small, quads * ch), BF16),
            pltpu.VMEM((chips, small, pair), F32),
            pltpu.VMEM((wide, small, pair), F32),
            pltpu.VMEM((fields, wide + 2, out_cols + 16, pair), F32),
            pltpu.VMEM((fields, 2 * place, taps * pair), BF16),
            pltpu.VMEM((fields * chips, own, place), F32),
            pltpu.VMEM((fields * line, own, place), F32),
            pltpu.VMEM((fields * line, own, place), F32),
            pltpu.VMEM((fields * line, own, place), F32),
            pltpu.VMEM((fields * chips, own, place), F32),
            pltpu.VMEM((fields, taps * pair, place), F32),
            pltpu.VMEM((fields, own, place), F32),
            pltpu.VMEM((fields, own, place), F32),
            dma((5,)), dma((2,)), dma((2,)), dma((2,)), dma((2,)),
            dma((wide,)), dma((wide,)), dma((fields * line,)), dma((fields * line,)),
            dma((fields * line,)), dma((fields * line,)), dma((fields * line,)), dma((fields * line,)),
            dma((fields * chips,)), dma((fields,)), dma((fields,)),
            pltpu.SemaphoreType.REGULAR((max(2, chips - 4),)), pltpu.SemaphoreType.REGULAR((2,)),
        ],
        compiler_params=pltpu.CompilerParams(
            collective_id=0, has_side_effects=True, vmem_limit_bytes=62 << 20
        ),
        cost_estimate=pl.CostEstimate(
            flops=2 * total * taps * full * full // chips, bytes_accessed=12 << 20, transcendentals=0
        ),
    )(features, first, down, inner, outer)


def fits(features, first_weight, down_weight, inner_weight):
    wide = lax.axis_size("wide")
    fields, rows, columns, ch = features.shape
    full = down_weight.shape[3]
    own = full // wide
    return (
        wide % 8 == 0 and rows == 2 and inner_weight.shape[0] == 1 and own % 64 == 0
        and 128 % own == 0 and full % 512 == 0 and ch % 128 == 0 and columns == 16
        and (wide * columns // 2) % 128 == 0 and fields * wide * columns <= 1024
    )


def choose(features, first_weight, down_weight, inner_weight, outer_weight):
    whole = fused_body if fits(features, first_weight, down_weight, inner_weight) else body
    return whole(features, first_weight, down_weight, inner_weight, outer_weight)


def solution(mesh):
    in_specs = (
        P("groups", "wide", None, None),
        P(),
        P(),
        P(None, None, None, None, "wide"),
        P(None, None, None, None, "wide"),
    )
    out_specs = P("groups", None, None, "wide")
    return jax.shard_map(choose, mesh=mesh, in_specs=in_specs, out_specs=out_specs, check_vma=False)
```

```python
import functools

import jax
import jax.numpy as jnp
from jax import lax
from jax.experimental import pallas as pl
from jax.experimental.pallas import tpu as pltpu
from jax.sharding import PartitionSpec as P


def extended_2(shard, sides, width):
    for axis, dim in sides:
        size, length = (lax.axis_size(axis), shard.shape[dim])
        up = [(i, (i + 1) % size) for i in range(size - 1)]
        down = [(j, i) for i, j in up]
        last = lax.slice_in_dim(shard, length - width, length, axis=dim)
        first = lax.slice_in_dim(shard, 0, width, axis=dim)
        before = lax.ppermute(last, axis, up)
        after = lax.ppermute(first, axis, down)
        shard = jnp.concatenate([before, shard, after], axis=dim)
    return shard


def partner_2(block, axis, distance):
    count = lax.axis_size(axis)
    route = []
    for low in range(count):
        high = low | 1 << distance
        if high != low and high < count:
            route += [(low, high), (high, low)]
    return lax.ppermute(block, axis, route)


def convolve(feature_map, kernel, layout, strides, padding):
    return lax.conv_general_dilated(
        feature_map,
        kernel,
        strides,
        padding,
        dimension_numbers=("NHWC", layout, "NHWC"),
        precision=lax.Precision.HIGHEST,
    )


def device_bit(bit_number):
    return lax.axis_index("wide") >> bit_number & 1


def spatial(local_rows, first_weight, down_weight):
    extended = extended_2(local_rows, (("wide", 1),), 1)
    activated = jax.nn.relu(convolve(extended, first_weight, "HWIO", (1, 1), [(0, 0), (1, 1)]))
    return convolve(activated, down_weight, "HWIO", (2, 2), "VALID")


def weight_blocks(stacked, grid_size, low_bits):
    leading = stacked.shape[:-2]
    width = stacked.shape[-2]
    narrow = stacked.shape[-1]
    slots = jnp.moveaxis(stacked.reshape(leading + (grid_size, width // grid_size, narrow)), -3, 0)
    remainder = slots.shape[1:]
    for bit_number in low_bits:
        paired = slots.reshape((grid_size >> bit_number + 1, 2, 1 << bit_number) + remainder)
        lower = paired[:, 0]
        upper = paired[:, 1]
        first_half = device_bit(bit_number) == 0
        outgoing = jnp.where(first_half, upper, lower)
        keeping = jnp.where(first_half, lower, upper)
        incoming = partner_2(outgoing, "wide", bit_number)
        merged = jnp.stack(
            [jnp.where(first_half, keeping, incoming), jnp.where(first_half, incoming, keeping)], 1
        )
        slots = merged.reshape((grid_size,) + remainder)
    joined = jnp.moveaxis(slots, 0, -2)
    return joined.reshape(leading + (width // grid_size, grid_size * narrow))


def channel_pieces(piece, low_bits):
    for bit_number in low_bits:
        partner = partner_2(piece, "wide", bit_number)
        first_half = device_bit(bit_number) == 0
        piece = jnp.where(
            first_half, jnp.concatenate([piece, partner], 3), jnp.concatenate([partner, piece], 3)
        )
    return piece


def group_total(partial_value, bit_list):
    for bit_number in bit_list:
        partial_value = partial_value + partner_2(partial_value, "wide", bit_number)
    return partial_value


def body(features, first_weight, down_weight, inner_weight, outer_weight):
    total_bits = lax.axis_size("wide").bit_length() - 1
    half_bits = total_bits // 2
    grid_size = 1 << half_bits
    low_bits = list(range(half_bits))
    high_bits = list(range(half_bits, total_bits))
    channels = down_weight.shape[3]
    stacked = weight_blocks(jnp.stack([inner_weight, outer_weight], 0), grid_size, low_bits)
    reduced = spatial(features, first_weight, down_weight)
    current = channel_pieces(
        lax.all_to_all(reduced, "wide", split_axis=3, concat_axis=1, tiled=True), low_bits
    )
    kernel_in = stacked[0, 0]
    kernel_out = stacked[1, 0]
    partial_value = convolve(current, kernel_in, "HWOI", (1, 1), "SAME")
    hidden = jax.nn.relu(group_total(partial_value, high_bits))
    partial_value = convolve(hidden, kernel_out, "HWIO", (1, 1), "SAME")
    current = jax.nn.relu(current + group_total(partial_value, low_bits))
    own_count = channels // lax.axis_size("wide")
    offset = lax.axis_index("wide") % grid_size * own_count
    return lax.dynamic_slice_in_dim(current, offset, own_count, 3)

MESH = pl.DeviceIdType.MESH
F32 = jnp.float32
BF16 = jnp.bfloat16


def halves(value):
    high = value.astype(BF16)
    return high, (value - high.astype(F32)).astype(BF16)


def dot(a, b):
    return jnp.dot(a, b, preferred_element_type=F32)


def fused(
    wide,
    feat_hbm, first_hbm, down_hbm, inner_hbm, outer_hbm, out_ref,
    feat, first, down, inner, outer,
    first_hi, first_lo, down_hi, down_lo, inner_hi, inner_lo, outer_all,
    halo, ext, cols1, act, cols2, red, gathered, ext2, cols3,
    part, from_y, to_z, from_z, hid, taps_out, mine, theirs,
    local_sem, halo_send, halo_recv, weight_send, weight_recv,
    a2a_send, a2a_recv, rsy_send, rsy_recv, rsz_send, rsz_recv, agy_send, agz_send, ag_recv,
    fin_send, fin_recv, relay, known,
):
    me = lax.axis_index("wide")
    core = lax.rem(me, 2)
    chip = lax.div(me, 2)
    mate = me + 1 - 2 * core
    chips = wide // 2
    line = chips // 2
    z = lax.div(chip, 2)
    y = lax.rem(chip, 2)
    across = me + 2 - 4 * y
    beside = me - 1 + 2 * core
    fields, rows, columns, ch = feat.shape
    own = inner.shape[2]
    half = inner.shape[3]
    pair = 2 * own
    out_cols = columns // 2
    field_pos = wide * out_cols
    block = inner_hi.shape[2]
    per_block = block // own
    blocks = half // block

    def remote(src, dst, send, recv, device):
        return pltpu.make_async_remote_copy(
            src_ref=src, dst_ref=dst, send_sem=send, recv_sem=recv,
            device_id={"wide": device}, device_id_type=MESH,
        )

    my_half = pl.ds(pl.multiple_of(core * half, half), half)
    mate_half = pl.ds(pl.multiple_of((1 - core) * half, half), half)
    local = [
        pltpu.make_async_copy(feat_hbm, feat, local_sem.at[0]),
        pltpu.make_async_copy(first_hbm, first, local_sem.at[1]),
        pltpu.make_async_copy(down_hbm, down, local_sem.at[2]),
        pltpu.make_async_copy(inner_hbm.at[:, :, my_half], inner.at[core], local_sem.at[3]),
        pltpu.make_async_copy(outer_hbm.at[:, :, my_half], outer.at[core], local_sem.at[4]),
    ]
    for copy in local:
        copy.start()

    barrier = pltpu.get_barrier_semaphore()
    has_below = z > 0
    has_above = z < line - 1
    has_beside = (beside >= 0) & (beside < wide)

    def signal(semaphore, device):
        pl.semaphore_signal(
            semaphore, inc=1, device_id={"wide": device}, device_id_type=MESH
        )

    signal(barrier, mate)
    signal(barrier, across)

    @pl.when(has_beside)
    def _():
        signal(barrier, beside)

    @pl.when(has_below)
    def _():
        signal(barrier, me - 4)

    @pl.when(has_above)
    def _():
        signal(barrier, me + 4)

    def relay_tell(r):
        @pl.when(has_above)
        def _():
            signal(relay.at[2 * r], me + 4)

        @pl.when(has_below)
        def _():
            signal(relay.at[2 * r + 1], me - 4)

    def relay_hear(r):
        @pl.when(has_below)
        def _():
            pl.semaphore_wait(relay.at[2 * r], 1)

        @pl.when(has_above)
        def _():
            pl.semaphore_wait(relay.at[2 * r + 1], 1)

    ext[...] = jnp.zeros_like(ext)
    ext2[...] = jnp.zeros_like(ext2)
    local[0].wait()
    greeted = (
        2 + has_beside.astype(jnp.int32) + has_below.astype(jnp.int32) + has_above.astype(jnp.int32)
    )
    pl.semaphore_wait(barrier, greeted)

    down_copy = remote(feat.at[:, rows - 1], halo.at[0], halo_send.at[0], halo_recv.at[0], me + 1)
    up_copy = remote(feat.at[:, 0], halo.at[1], halo_send.at[1], halo_recv.at[1], me - 1)

    @pl.when(me < wide - 1)
    def _():
        down_copy.start()

    @pl.when(me > 0)
    def _():
        up_copy.start()

    swap = [
        remote(inner_hbm.at[:, :, mate_half], inner.at[core], weight_send.at[0], weight_recv.at[0], mate),
        remote(outer_hbm.at[:, :, mate_half], outer.at[core], weight_send.at[1], weight_recv.at[1], mate),
    ]
    for copy in swap:
        copy.start()

    def prepare_down():
        for t in range(down.shape[0]):
            high, low = halves(down[t])
            down_hi[t * ch : (t + 1) * ch, :] = high
            down_lo[t * ch : (t + 1) * ch, :] = low

    rounds = line - 2
    if rounds:
        relay_tell(0)
    ext[:, 1 : rows + 1, 8 : 8 + columns, :] = feat[...]
    local[1].wait()
    taps = first.shape[0]
    for t in range(taps):
        high, low = halves(first[t])
        first_hi[t * ch : (t + 1) * ch, :] = high
        first_lo[t * ch : (t + 1) * ch, :] = low
    for r in range(rounds):
        relay_hear(r)
        if r + 1 < rounds:
            relay_tell(r + 1)
        if r == 0:
            local[2].wait()
            prepare_down()
    if not rounds:
        local[2].wait()
        prepare_down()
    signal(known.at[0], across)

    @pl.when(me > 0)
    def _():
        down_copy.wait_recv()
        ext[:, 0, 8 : 8 + columns, :] = halo[0]

    @pl.when(me < wide - 1)
    def _():
        up_copy.wait_recv()
        ext[:, rows + 1, 8 : 8 + columns, :] = halo[1]

    pl.semaphore_wait(known.at[0], 1)
    signal(known.at[1], mate)
    count = fields * rows * columns
    for t in range(taps):
        dr, dc = divmod(t, 3)
        slab = ext[:, dr : dr + rows, 7 + dc : 7 + dc + columns, :].reshape(count, ch)
        high, low = halves(slab)
        cols1[0:count, t * ch : (t + 1) * ch] = high
        cols1[count : 2 * count, t * ch : (t + 1) * ch] = low
    both = dot(cols1[...], first_hi[...])
    activated = both[0:count] + both[count : 2 * count] + dot(cols1[0:count, :], first_lo[...])
    activated = jnp.maximum(activated, 0.0)
    lanes = act.shape[2]
    for piece in range(ch // lanes):
        act[piece] = activated[:, piece * lanes : (piece + 1) * lanes]
    small = fields * out_cols
    for t in range(down.shape[0]):
        dr, dc = divmod(t, 2)
        for piece in range(ch // lanes):
            got = jnp.concatenate(
                [
                    act[piece, pl.ds((f * rows + dr) * columns + dc, out_cols, stride=2), :]
                    for f in range(fields)
                ],
                axis=0,
            )
            high, low = halves(got)
            at = t * ch + piece * lanes
            cols2[0:small, at : at + lanes] = high
            cols2[small : 2 * small, at : at + lanes] = low
    both = dot(cols2[...], down_hi[...])
    reduced = both[0:small] + both[small : 2 * small] + dot(cols2[0:small, :], down_lo[...])
    for c in range(chips):
        red[c] = reduced[:, c * pair : (c + 1) * pair]

    def a2a(k):
        to = lax.rem(me + k, wide)
        return remote(red.at[lax.div(to, 2)], gathered.at[me], a2a_send.at[k], a2a_recv.at[me], to)

    def a2a_start(k, carry):
        a2a(1 + lax.rem(k + wide // 2 - 3, wide - 1)).start()
        return carry

    pl.semaphore_wait(known.at[1], 1)
    lax.fori_loop(1, wide, a2a_start, 0)
    gathered[me] = red[chip]

    local[3].wait()
    swap[0].wait_recv()
    for t in range(taps):
        for q in range(2):
            high, low = halves(inner[q, t])
            at = t * pair + q * own
            for b in range(blocks):
                inner_hi[b, at : at + own, :] = high[:, b * block : (b + 1) * block]
                inner_lo[b, at : at + own, :] = low[:, b * block : (b + 1) * block]

    local[4].wait()
    swap[1].wait_recv()
    span = taps * pair
    for t in range(taps):
        for q in range(2):
            high, low = halves(outer[q, t])
            at = t * pair + q * own
            for b in range(blocks):
                outer_all[b, at : at + own, :] = high[:, b * block : (b + 1) * block]
                outer_all[b, span + at : span + at + own, :] = low[:, b * block : (b + 1) * block]

    def a2a_wait(k, carry):
        source = lax.rem(me + k, wide)
        remote(red.at[0], gathered.at[source], a2a_send.at[k], a2a_recv.at[source], source).wait_recv()
        return carry

    lax.fori_loop(1, wide, a2a_wait, 0)

    for f in range(fields):
        ext2[f, 1 : wide + 1, 8 : 8 + out_cols, :] = gathered[:, f * out_cols : (f + 1) * out_cols, :]
    my_block = lax.div(chip, per_block)
    half_block = per_block // 2

    def rs_y(f, zz):
        at = f * line + zz
        return remote(
            part.at[f * chips + 2 * zz + 1 - y], from_y.at[at], rsy_send.at[at], rsy_recv.at[at], across
        )

    def rs_z(f, zz):
        at = f * line
        return remote(
            to_z.at[at + zz], from_z.at[at + z], rsz_send.at[at + zz], rsz_recv.at[at + z],
            4 * zz + 2 * y + core,
        )

    for f in range(fields):
        for t in range(taps):
            dr, dc = divmod(t, 3)
            slab = ext2[f, dr : dr + wide, 7 + dc : 7 + dc + out_cols, :].reshape(field_pos, pair)
            high, low = halves(slab)
            cols3[f, 0:field_pos, t * pair : (t + 1) * pair] = high
            cols3[f, field_pos : 2 * field_pos, t * pair : (t + 1) * pair] = low
        for step in range(blocks):
            b = lax.rem(my_block + step + 1, blocks)
            both = dot(cols3[f], inner_hi[b])
            value = both[0:field_pos] + both[field_pos:] + dot(cols3[f, 0:field_pos, :], inner_lo[b])
            turned = value.T
            for j in range(per_block):
                part[f * chips + b * per_block + j] = turned[j * own : (j + 1) * own]
            for j in range(half_block):
                rs_y(f, b * half_block + j).start()

    def pass_on(f):
        for step in range(blocks):
            b = lax.rem(my_block + step + 1, blocks)
            for j in range(half_block):
                zz = b * half_block + j
                rs_y(f, zz).wait_recv()
                to_z[f * line + zz] = part[f * chips + 2 * zz + y] + from_y[f * line + zz]

                @pl.when(zz != z)
                def _():
                    rs_z(f, zz).start()

    for f in range(fields):
        pass_on(f)

    def ag_z(f, zz):
        at = f * chips + chip
        return remote(
            hid.at[at], hid.at[at], agz_send.at[f * line + zz], ag_recv.at[at], 4 * zz + 2 * y + core
        )

    def ag_y(f, zz):
        at = f * chips + 2 * zz + y
        return remote(hid.at[at], hid.at[at], agy_send.at[f * line + zz], ag_recv.at[at], across)

    def arrived(f, c, device):
        at = f * chips + c
        remote(hid.at[at], hid.at[at], agz_send.at[0], ag_recv.at[at], device).wait_recv()

    def collect(f):
        hidden = to_z[f * line + z]
        for k in range(1, line):
            source = lax.rem(z + k, line)
            at = f * line + source
            remote(
                to_z.at[0], from_z.at[at], rsz_send.at[at], rsz_recv.at[at], 4 * source + 2 * y + core
            ).wait_recv()
            hidden = hidden + from_z[at]
        hid[f * chips + chip] = jnp.maximum(hidden, 0.0)
        for step in range(blocks):
            b = lax.rem(my_block + step + 1, blocks)
            for j in range(half_block):
                zz = b * half_block + j

                @pl.when(zz != z)
                def _():
                    ag_z(f, zz).start()

        ag_y(f, z).start()

    def forward(f, step):
        b = lax.rem(my_block + step, blocks)
        for j in range(half_block):
            zz = b * half_block + j

            @pl.when(zz != z)
            def _():
                arrived(f, 2 * zz + y, 4 * zz + 2 * y + core)
                ag_y(f, zz).start()

    def multiply(f, step):
        b = lax.rem(my_block + step, blocks)
        for j in range(half_block):
            arrived(f, 2 * (b * half_block + j) + 1 - y, across)
        gained = hid[pl.ds(f * chips + b * per_block, per_block)].reshape(block, field_pos)
        high, low = halves(gained)
        both = dot(outer_all[b], high)
        value = both[0:span] + both[span : 2 * span] + dot(outer_all[b, 0:span, :], low)
        if step == 0:
            taps_out[f] = value
        else:
            taps_out[f] += value

    place = lax.broadcasted_iota(jnp.int32, (own, field_pos), 1)
    row = lax.div(place, out_cols)
    col = lax.rem(place, out_cols)

    def shifted(q, f):
        total_value = jnp.zeros((own, field_pos), F32)
        for t in range(taps):
            dr, dc = divmod(t, 3)
            dr, dc = dr - 1, dc - 1
            at = pl.multiple_of(t * pair + q * own, own)
            value = taps_out[f, pl.ds(at, own), :]
            offset = dr * out_cols + dc
            if offset:
                value = pltpu.roll(value, (-offset) % field_pos, 1)
                good = (row + dr >= 0) & (row + dr < wide) & (col + dc >= 0) & (col + dc < out_cols)
                value = jnp.where(good, value, 0.0)
            total_value = total_value + value
        return total_value

    def last(f):
        return remote(mine.at[f], theirs.at[f], fin_send.at[f], fin_recv.at[f], mate)

    def give(f):
        mine[f] = shifted(1 - core, f)
        last(f).start()

    for f in range(fields):
        collect(f)
    for step in range(blocks):
        forward(0, step)
    for f in range(fields):
        for step in range(blocks):
            multiply(f, step)
            if f + 1 < fields:
                forward(f + 1, step)
        give(f)
    for f in range(fields):
        kept = shifted(core, f)
        last(f).wait_recv()
        value = (kept + theirs[f]).T
        before = ext2[f, 1 : wide + 1, 8 : 8 + out_cols, :].reshape(field_pos, pair)
        before = jnp.where(core == 0, before[:, 0:own], before[:, own:pair])
        out_ref[f] = jnp.maximum(before + value, 0.0).reshape(wide, out_cols, own)

    @pl.when(me < wide - 1)
    def _():
        down_copy.wait_send()

    @pl.when(me > 0)
    def _():
        up_copy.wait_send()

    for copy in swap:
        copy.wait_send()

    def a2a_done(k, carry):
        a2a(k).wait_send()
        return carry

    lax.fori_loop(1, wide, a2a_done, 0)

    for f in range(fields):
        last(f).wait_send()
        for zz in range(line):
            rs_y(f, zz).wait_send()
            ag_y(f, zz).wait_send()

            @pl.when(zz != z)
            def _():
                rs_z(f, zz).wait_send()
                ag_z(f, zz).wait_send()


def fused_body(features, first_weight, down_weight, inner_weight, outer_weight):
    wide = lax.axis_size("wide")
    chips = wide // 2
    fields, rows, columns, ch = features.shape
    full = down_weight.shape[3]
    own = full // wide
    pair, half = 2 * own, full // 2
    taps, quads = 9, 4
    out_cols = columns // 2
    place, line = wide * out_cols, chips // 2
    total = fields * place
    count, small = fields * rows * columns, fields * out_cols
    block = 256
    blocks = half // block
    first = first_weight.reshape(taps, ch, ch)
    down = down_weight.reshape(quads, ch, full)
    inner = jnp.swapaxes(inner_weight, 3, 4).reshape(taps, own, full)
    outer = jnp.swapaxes(outer_weight, 3, 4).reshape(taps, own, full)
    dma = pltpu.SemaphoreType.DMA
    return pl.pallas_call(
        functools.partial(fused, wide),
        out_shape=jax.ShapeDtypeStruct((fields, wide, out_cols, own), F32),
        in_specs=[pl.BlockSpec(memory_space=pl.ANY)] * 5,
        out_specs=pl.BlockSpec(memory_space=pltpu.VMEM),
        scratch_shapes=[
            pltpu.VMEM(features.shape, F32),
            pltpu.VMEM((taps, ch, ch), F32),
            pltpu.VMEM((quads, ch, full), F32),
            pltpu.VMEM((2, taps, own, half), F32),
            pltpu.VMEM((2, taps, own, half), F32),
            pltpu.VMEM((taps * ch, ch), BF16),
            pltpu.VMEM((taps * ch, ch), BF16),
            pltpu.VMEM((quads * ch, full), BF16),
            pltpu.VMEM((quads * ch, full), BF16),
            pltpu.VMEM((blocks, taps * pair, block), BF16),
            pltpu.VMEM((blocks, taps * pair, block), BF16),
            pltpu.VMEM((blocks, 2 * taps * pair, block), BF16),
            pltpu.VMEM((2, fields, columns, ch), F32),
            pltpu.VMEM((fields, rows + 2, columns + 16, ch), F32),
            pltpu.VMEM((2 * count, taps * ch), BF16),
            pltpu.VMEM((ch // 128, count, 128), F32),
            pltpu.VMEM((2 * small, quads * ch), BF16),
            pltpu.VMEM((chips, small, pair), F32),
            pltpu.VMEM((wide, small, pair), F32),
            pltpu.VMEM((fields, wide + 2, out_cols + 16, pair), F32),
            pltpu.VMEM((fields, 2 * place, taps * pair), BF16),
            pltpu.VMEM((fields * chips, own, place), F32),
            pltpu.VMEM((fields * line, own, place), F32),
            pltpu.VMEM((fields * line, own, place), F32),
            pltpu.VMEM((fields * line, own, place), F32),
            pltpu.VMEM((fields * chips, own, place), F32),
            pltpu.VMEM((fields, taps * pair, place), F32),
            pltpu.VMEM((fields, own, place), F32),
            pltpu.VMEM((fields, own, place), F32),
            dma((5,)), dma((2,)), dma((2,)), dma((2,)), dma((2,)),
            dma((wide,)), dma((wide,)), dma((fields * line,)), dma((fields * line,)),
            dma((fields * line,)), dma((fields * line,)), dma((fields * line,)), dma((fields * line,)),
            dma((fields * chips,)), dma((fields,)), dma((fields,)),
            pltpu.SemaphoreType.REGULAR((max(2, chips - 4),)), pltpu.SemaphoreType.REGULAR((2,)),
        ],
        compiler_params=pltpu.CompilerParams(
            collective_id=0, has_side_effects=True, vmem_limit_bytes=62 << 20
        ),
        cost_estimate=pl.CostEstimate(
            flops=2 * total * taps * full * full // chips, bytes_accessed=12 << 20, transcendentals=0
        ),
    )(features, first, down, inner, outer)


def fits(features, first_weight, down_weight, inner_weight):
    wide = lax.axis_size("wide")
    fields, rows, columns, ch = features.shape
    full = down_weight.shape[3]
    own = full // wide
    return (
        wide % 8 == 0 and rows == 2 and inner_weight.shape[0] == 1 and own % 64 == 0
        and 128 % own == 0 and full % 512 == 0 and ch % 128 == 0 and columns == 16
        and (wide * columns // 2) % 128 == 0 and fields * wide * columns <= 1024
    )


def choose(features, first_weight, down_weight, inner_weight, outer_weight):
    whole = fused_body if fits(features, first_weight, down_weight, inner_weight) else body
    return whole(features, first_weight, down_weight, inner_weight, outer_weight)


def solution(mesh):
    in_specs = (
        P("groups", "wide", None, None),
        P(),
        P(),
        P(None, None, None, None, "wide"),
        P(None, None, None, None, "wide"),
    )
    out_specs = P("groups", None, None, "wide")
    return jax.shard_map(choose, mesh=mesh, in_specs=in_specs, out_specs=out_specs, check_vma=False)
```

```python
import functools

import jax
import jax.numpy as jnp
from jax import lax
from jax.experimental import pallas as pl
from jax.experimental.pallas import tpu as pltpu
from jax.sharding import PartitionSpec as P


def extended_2(shard, sides, width):
    for axis, dim in sides:
        size, length = (lax.axis_size(axis), shard.shape[dim])
        up = [(i, (i + 1) % size) for i in range(size - 1)]
        down = [(j, i) for i, j in up]
        last = lax.slice_in_dim(shard, length - width, length, axis=dim)
        first = lax.slice_in_dim(shard, 0, width, axis=dim)
        before = lax.ppermute(last, axis, up)
        after = lax.ppermute(first, axis, down)
        shard = jnp.concatenate([before, shard, after], axis=dim)
    return shard


def partner_2(block, axis, distance):
    count = lax.axis_size(axis)
    route = []
    for low in range(count):
        high = low | 1 << distance
        if high != low and high < count:
            route += [(low, high), (high, low)]
    return lax.ppermute(block, axis, route)


def convolve(feature_map, kernel, layout, strides, padding):
    return lax.conv_general_dilated(
        feature_map,
        kernel,
        strides,
        padding,
        dimension_numbers=("NHWC", layout, "NHWC"),
        precision=lax.Precision.HIGHEST,
    )


def device_bit(bit_number):
    return lax.axis_index("wide") >> bit_number & 1


def spatial(local_rows, first_weight, down_weight):
    extended = extended_2(local_rows, (("wide", 1),), 1)
    activated = jax.nn.relu(convolve(extended, first_weight, "HWIO", (1, 1), [(0, 0), (1, 1)]))
    return convolve(activated, down_weight, "HWIO", (2, 2), "VALID")


def weight_blocks(stacked, grid_size, low_bits):
    leading = stacked.shape[:-2]
    width = stacked.shape[-2]
    narrow = stacked.shape[-1]
    slots = jnp.moveaxis(stacked.reshape(leading + (grid_size, width // grid_size, narrow)), -3, 0)
    remainder = slots.shape[1:]
    for bit_number in low_bits:
        paired = slots.reshape((grid_size >> bit_number + 1, 2, 1 << bit_number) + remainder)
        lower = paired[:, 0]
        upper = paired[:, 1]
        first_half = device_bit(bit_number) == 0
        outgoing = jnp.where(first_half, upper, lower)
        keeping = jnp.where(first_half, lower, upper)
        incoming = partner_2(outgoing, "wide", bit_number)
        merged = jnp.stack(
            [jnp.where(first_half, keeping, incoming), jnp.where(first_half, incoming, keeping)], 1
        )
        slots = merged.reshape((grid_size,) + remainder)
    joined = jnp.moveaxis(slots, 0, -2)
    return joined.reshape(leading + (width // grid_size, grid_size * narrow))


def channel_pieces(piece, low_bits):
    for bit_number in low_bits:
        partner = partner_2(piece, "wide", bit_number)
        first_half = device_bit(bit_number) == 0
        piece = jnp.where(
            first_half, jnp.concatenate([piece, partner], 3), jnp.concatenate([partner, piece], 3)
        )
    return piece


def group_total(partial_value, bit_list):
    for bit_number in bit_list:
        partial_value = partial_value + partner_2(partial_value, "wide", bit_number)
    return partial_value


def body(features, first_weight, down_weight, inner_weight, outer_weight):
    total_bits = lax.axis_size("wide").bit_length() - 1
    half_bits = total_bits // 2
    grid_size = 1 << half_bits
    low_bits = list(range(half_bits))
    high_bits = list(range(half_bits, total_bits))
    channels = down_weight.shape[3]
    stacked = weight_blocks(jnp.stack([inner_weight, outer_weight], 0), grid_size, low_bits)
    reduced = spatial(features, first_weight, down_weight)
    current = channel_pieces(
        lax.all_to_all(reduced, "wide", split_axis=3, concat_axis=1, tiled=True), low_bits
    )
    kernel_in = stacked[0, 0]
    kernel_out = stacked[1, 0]
    partial_value = convolve(current, kernel_in, "HWOI", (1, 1), "SAME")
    hidden = jax.nn.relu(group_total(partial_value, high_bits))
    partial_value = convolve(hidden, kernel_out, "HWIO", (1, 1), "SAME")
    current = jax.nn.relu(current + group_total(partial_value, low_bits))
    own_count = channels // lax.axis_size("wide")
    offset = lax.axis_index("wide") % grid_size * own_count
    return lax.dynamic_slice_in_dim(current, offset, own_count, 3)

MESH = pl.DeviceIdType.MESH
F32 = jnp.float32
BF16 = jnp.bfloat16


def halves(value):
    high = value.astype(BF16)
    return high, (value - high.astype(F32)).astype(BF16)


def dot(a, b):
    return jnp.dot(a, b, preferred_element_type=F32)


def fused(
    wide,
    feat_hbm, first_hbm, down_hbm, inner_hbm, outer_hbm, out_ref,
    feat, first, down, inner, outer,
    first_hi, first_lo, down_hi, down_lo, inner_hi, inner_lo, outer_all,
    halo, ext, cols1, act, cols2, red, gathered, ext2, cols3,
    part, from_y, to_z, from_z, hid, taps_out, mine, theirs,
    local_sem, halo_send, halo_recv, weight_send, weight_recv,
    a2a_send, a2a_recv, rsy_send, rsy_recv, rsz_send, rsz_recv, agy_send, agz_send, ag_recv,
    fin_send, fin_recv, relay, known,
):
    me = lax.axis_index("wide")
    core = lax.rem(me, 2)
    chip = lax.div(me, 2)
    mate = me + 1 - 2 * core
    chips = wide // 2
    line = chips // 2
    z = lax.div(chip, 2)
    y = lax.rem(chip, 2)
    across = me + 2 - 4 * y
    beside = me - 1 + 2 * core
    fields, rows, columns, ch = feat.shape
    own = inner.shape[2]
    half = inner.shape[3]
    pair = 2 * own
    out_cols = columns // 2
    field_pos = wide * out_cols
    block = inner_hi.shape[2]
    per_block = block // own
    blocks = half // block

    def remote(src, dst, send, recv, device):
        return pltpu.make_async_remote_copy(
            src_ref=src, dst_ref=dst, send_sem=send, recv_sem=recv,
            device_id={"wide": device}, device_id_type=MESH,
        )

    my_half = pl.ds(pl.multiple_of(core * half, half), half)
    mate_half = pl.ds(pl.multiple_of((1 - core) * half, half), half)
    local = [
        pltpu.make_async_copy(feat_hbm, feat, local_sem.at[0]),
        pltpu.make_async_copy(first_hbm, first, local_sem.at[1]),
        pltpu.make_async_copy(down_hbm, down, local_sem.at[2]),
        pltpu.make_async_copy(inner_hbm.at[:, :, my_half], inner.at[core], local_sem.at[3]),
        pltpu.make_async_copy(outer_hbm.at[:, :, my_half], outer.at[core], local_sem.at[4]),
    ]
    for copy in local:
        copy.start()

    barrier = pltpu.get_barrier_semaphore()
    has_below = z > 0
    has_above = z < line - 1
    has_beside = (beside >= 0) & (beside < wide)

    def signal(semaphore, device):
        pl.semaphore_signal(
            semaphore, inc=1, device_id={"wide": device}, device_id_type=MESH
        )

    signal(barrier, mate)
    signal(barrier, across)

    @pl.when(has_beside)
    def _():
        signal(barrier, beside)

    @pl.when(has_below)
    def _():
        signal(barrier, me - 4)

    @pl.when(has_above)
    def _():
        signal(barrier, me + 4)

    def relay_tell(r):
        @pl.when(has_above)
        def _():
            signal(relay.at[2 * r], me + 4)

        @pl.when(has_below)
        def _():
            signal(relay.at[2 * r + 1], me - 4)

    def relay_hear(r):
        @pl.when(has_below)
        def _():
            pl.semaphore_wait(relay.at[2 * r], 1)

        @pl.when(has_above)
        def _():
            pl.semaphore_wait(relay.at[2 * r + 1], 1)

    ext[...] = jnp.zeros_like(ext)
    ext2[...] = jnp.zeros_like(ext2)
    local[0].wait()
    greeted = (
        2 + has_beside.astype(jnp.int32) + has_below.astype(jnp.int32) + has_above.astype(jnp.int32)
    )
    pl.semaphore_wait(barrier, greeted)

    down_copy = remote(feat.at[:, rows - 1], halo.at[0], halo_send.at[0], halo_recv.at[0], me + 1)
    up_copy = remote(feat.at[:, 0], halo.at[1], halo_send.at[1], halo_recv.at[1], me - 1)

    @pl.when(me < wide - 1)
    def _():
        down_copy.start()

    @pl.when(me > 0)
    def _():
        up_copy.start()

    swap = [
        remote(inner_hbm.at[:, :, mate_half], inner.at[core], weight_send.at[0], weight_recv.at[0], mate),
        remote(outer_hbm.at[:, :, mate_half], outer.at[core], weight_send.at[1], weight_recv.at[1], mate),
    ]
    for copy in swap:
        copy.start()

    def prepare_down():
        for t in range(down.shape[0]):
            high, low = halves(down[t])
            down_hi[t * ch : (t + 1) * ch, :] = high
            down_lo[t * ch : (t + 1) * ch, :] = low

    rounds = line - 2
    if rounds:
        relay_tell(0)
    ext[:, 1 : rows + 1, 8 : 8 + columns, :] = feat[...]
    local[1].wait()
    taps = first.shape[0]
    for t in range(taps):
        high, low = halves(first[t])
        first_hi[t * ch : (t + 1) * ch, :] = high
        first_lo[t * ch : (t + 1) * ch, :] = low
    for r in range(rounds):
        relay_hear(r)
        if r + 1 < rounds:
            relay_tell(r + 1)
        if r == 0:
            local[2].wait()
            prepare_down()
    if not rounds:
        local[2].wait()
        prepare_down()
    signal(known.at[0], across)

    @pl.when(me > 0)
    def _():
        down_copy.wait_recv()
        ext[:, 0, 8 : 8 + columns, :] = halo[0]

    @pl.when(me < wide - 1)
    def _():
        up_copy.wait_recv()
        ext[:, rows + 1, 8 : 8 + columns, :] = halo[1]

    pl.semaphore_wait(known.at[0], 1)
    signal(known.at[1], mate)
    count = fields * rows * columns
    for t in range(taps):
        dr, dc = divmod(t, 3)
        slab = ext[:, dr : dr + rows, 7 + dc : 7 + dc + columns, :].reshape(count, ch)
        high, low = halves(slab)
        cols1[0:count, t * ch : (t + 1) * ch] = high
        cols1[count : 2 * count, t * ch : (t + 1) * ch] = low
    both = dot(cols1[...], first_hi[...])
    activated = both[0:count] + both[count : 2 * count] + dot(cols1[0:count, :], first_lo[...])
    activated = jnp.maximum(activated, 0.0)
    lanes = act.shape[2]
    for piece in range(ch // lanes):
        act[piece] = activated[:, piece * lanes : (piece + 1) * lanes]
    small = fields * out_cols
    for t in range(down.shape[0]):
        dr, dc = divmod(t, 2)
        for piece in range(ch // lanes):
            got = jnp.concatenate(
                [
                    act[piece, pl.ds((f * rows + dr) * columns + dc, out_cols, stride=2), :]
                    for f in range(fields)
                ],
                axis=0,
            )
            high, low = halves(got)
            at = t * ch + piece * lanes
            cols2[0:small, at : at + lanes] = high
            cols2[small : 2 * small, at : at + lanes] = low
    both = dot(cols2[...], down_hi[...])
    reduced = both[0:small] + both[small : 2 * small] + dot(cols2[0:small, :], down_lo[...])
    for c in range(chips):
        red[c] = reduced[:, c * pair : (c + 1) * pair]

    def a2a(k):
        to = lax.rem(me + k, wide)
        return remote(red.at[lax.div(to, 2)], gathered.at[me], a2a_send.at[k], a2a_recv.at[me], to)

    def a2a_start(k, carry):
        a2a(1 + lax.rem(k + wide // 2 - 3, wide - 1)).start()
        return carry

    pl.semaphore_wait(known.at[1], 1)
    lax.fori_loop(1, wide, a2a_start, 0)
    gathered[me] = red[chip]

    local[3].wait()
    swap[0].wait_recv()
    for t in range(taps):
        for q in range(2):
            high, low = halves(inner[q, t])
            at = t * pair + q * own
            for b in range(blocks):
                inner_hi[b, at : at + own, :] = high[:, b * block : (b + 1) * block]
                inner_lo[b, at : at + own, :] = low[:, b * block : (b + 1) * block]

    local[4].wait()
    swap[1].wait_recv()
    span = taps * pair
    for t in range(taps):
        for q in range(2):
            high, low = halves(outer[q, t])
            at = t * pair + q * own
            for b in range(blocks):
                outer_all[b, at : at + own, :] = high[:, b * block : (b + 1) * block]
                outer_all[b, span + at : span + at + own, :] = low[:, b * block : (b + 1) * block]

    def a2a_wait(k, carry):
        source = lax.rem(me + k, wide)
        remote(red.at[0], gathered.at[source], a2a_send.at[k], a2a_recv.at[source], source).wait_recv()
        return carry

    lax.fori_loop(1, wide, a2a_wait, 0)

    for f in range(fields):
        ext2[f, 1 : wide + 1, 8 : 8 + out_cols, :] = gathered[:, f * out_cols : (f + 1) * out_cols, :]
    my_block = lax.div(chip, per_block)
    half_block = per_block // 2

    def rs_y(f, zz):
        at = f * line + zz
        return remote(
            part.at[f * chips + 2 * zz + 1 - y], from_y.at[at], rsy_send.at[at], rsy_recv.at[at], across
        )

    def rs_z(f, zz):
        at = f * line
        return remote(
            to_z.at[at + zz], from_z.at[at + z], rsz_send.at[at + zz], rsz_recv.at[at + z],
            4 * zz + 2 * y + core,
        )

    for f in range(fields):
        for t in range(taps):
            dr, dc = divmod(t, 3)
            slab = ext2[f, dr : dr + wide, 7 + dc : 7 + dc + out_cols, :].reshape(field_pos, pair)
            high, low = halves(slab)
            cols3[f, 0:field_pos, t * pair : (t + 1) * pair] = high
            cols3[f, field_pos : 2 * field_pos, t * pair : (t + 1) * pair] = low
        for step in range(blocks):
            b = lax.rem(my_block + step + 1, blocks)
            both = dot(cols3[f], inner_hi[b])
            value = both[0:field_pos] + both[field_pos:] + dot(cols3[f, 0:field_pos, :], inner_lo[b])
            turned = value.T
            for j in range(per_block):
                part[f * chips + b * per_block + j] = turned[j * own : (j + 1) * own]
            for j in range(half_block):
                rs_y(f, b * half_block + j).start()

    def pass_on(f):
        for step in range(blocks):
            b = lax.rem(my_block + step + 1, blocks)
            for j in range(half_block):
                zz = b * half_block + j
                rs_y(f, zz).wait_recv()
                to_z[f * line + zz] = part[f * chips + 2 * zz + y] + from_y[f * line + zz]

                @pl.when(zz != z)
                def _():
                    rs_z(f, zz).start()

    for f in range(fields):
        pass_on(f)

    def ag_z(f, zz):
        at = f * chips + chip
        return remote(
            hid.at[at], hid.at[at], agz_send.at[f * line + zz], ag_recv.at[at], 4 * zz + 2 * y + core
        )

    def ag_y(f, zz):
        at = f * chips + 2 * zz + y
        return remote(hid.at[at], hid.at[at], agy_send.at[f * line + zz], ag_recv.at[at], across)

    def arrived(f, c, device):
        at = f * chips + c
        remote(hid.at[at], hid.at[at], agz_send.at[0], ag_recv.at[at], device).wait_recv()

    def collect(f):
        hidden = to_z[f * line + z]
        for k in range(1, line):
            source = lax.rem(z + k, line)
            at = f * line + source
            remote(
                to_z.at[0], from_z.at[at], rsz_send.at[at], rsz_recv.at[at], 4 * source + 2 * y + core
            ).wait_recv()
            hidden = hidden + from_z[at]
        hid[f * chips + chip] = jnp.maximum(hidden, 0.0)
        for step in range(blocks):
            b = lax.rem(my_block + step + 1, blocks)
            for j in range(half_block):
                zz = b * half_block + j

                @pl.when(zz != z)
                def _():
                    ag_z(f, zz).start()

        ag_y(f, z).start()

    def forward(f, step):
        b = lax.rem(my_block + step, blocks)
        for j in range(half_block):
            zz = b * half_block + j

            @pl.when(zz != z)
            def _():
                arrived(f, 2 * zz + y, 4 * zz + 2 * y + core)
                ag_y(f, zz).start()

    def multiply(f, step):
        b = lax.rem(my_block + step, blocks)
        for j in range(half_block):
            arrived(f, 2 * (b * half_block + j) + 1 - y, across)
        gained = hid[pl.ds(f * chips + b * per_block, per_block)].reshape(block, field_pos)
        high, low = halves(gained)
        both = dot(outer_all[b], high)
        value = both[0:span] + both[span : 2 * span] + dot(outer_all[b, 0:span, :], low)
        if step == 0:
            taps_out[f] = value
        else:
            taps_out[f] += value

    place = lax.broadcasted_iota(jnp.int32, (own, field_pos), 1)
    row = lax.div(place, out_cols)
    col = lax.rem(place, out_cols)

    def shifted(q, f):
        total_value = jnp.zeros((own, field_pos), F32)
        for t in range(taps):
            dr, dc = divmod(t, 3)
            dr, dc = dr - 1, dc - 1
            at = pl.multiple_of(t * pair + q * own, own)
            value = taps_out[f, pl.ds(at, own), :]
            offset = dr * out_cols + dc
            if offset:
                value = pltpu.roll(value, (-offset) % field_pos, 1)
                good = (row + dr >= 0) & (row + dr < wide) & (col + dc >= 0) & (col + dc < out_cols)
                value = jnp.where(good, value, 0.0)
            total_value = total_value + value
        return total_value

    def last(f):
        return remote(mine.at[f], theirs.at[f], fin_send.at[f], fin_recv.at[f], mate)

    def give(f):
        mine[f] = shifted(1 - core, f)
        last(f).start()

    collect(0)
    forward(0, 0)
    for f in range(1, fields):
        collect(f)
    for step in range(1, blocks):
        forward(0, step)
    for f in range(fields):
        for step in range(blocks):
            multiply(f, step)
            if f + 1 < fields:
                forward(f + 1, step)
        give(f)
    for f in range(fields):
        kept = shifted(core, f)
        last(f).wait_recv()
        value = (kept + theirs[f]).T
        before = ext2[f, 1 : wide + 1, 8 : 8 + out_cols, :].reshape(field_pos, pair)
        before = jnp.where(core == 0, before[:, 0:own], before[:, own:pair])
        out_ref[f] = jnp.maximum(before + value, 0.0).reshape(wide, out_cols, own)

    @pl.when(me < wide - 1)
    def _():
        down_copy.wait_send()

    @pl.when(me > 0)
    def _():
        up_copy.wait_send()

    for copy in swap:
        copy.wait_send()

    def a2a_done(k, carry):
        a2a(k).wait_send()
        return carry

    lax.fori_loop(1, wide, a2a_done, 0)

    for f in range(fields):
        last(f).wait_send()
        for zz in range(line):
            rs_y(f, zz).wait_send()
            ag_y(f, zz).wait_send()

            @pl.when(zz != z)
            def _():
                rs_z(f, zz).wait_send()
                ag_z(f, zz).wait_send()


def fused_body(features, first_weight, down_weight, inner_weight, outer_weight):
    wide = lax.axis_size("wide")
    chips = wide // 2
    fields, rows, columns, ch = features.shape
    full = down_weight.shape[3]
    own = full // wide
    pair, half = 2 * own, full // 2
    taps, quads = 9, 4
    out_cols = columns // 2
    place, line = wide * out_cols, chips // 2
    total = fields * place
    count, small = fields * rows * columns, fields * out_cols
    block = 256
    blocks = half // block
    first = first_weight.reshape(taps, ch, ch)
    down = down_weight.reshape(quads, ch, full)
    inner = jnp.swapaxes(inner_weight, 3, 4).reshape(taps, own, full)
    outer = jnp.swapaxes(outer_weight, 3, 4).reshape(taps, own, full)
    dma = pltpu.SemaphoreType.DMA
    return pl.pallas_call(
        functools.partial(fused, wide),
        out_shape=jax.ShapeDtypeStruct((fields, wide, out_cols, own), F32),
        in_specs=[pl.BlockSpec(memory_space=pl.ANY)] * 5,
        out_specs=pl.BlockSpec(memory_space=pltpu.VMEM),
        scratch_shapes=[
            pltpu.VMEM(features.shape, F32),
            pltpu.VMEM((taps, ch, ch), F32),
            pltpu.VMEM((quads, ch, full), F32),
            pltpu.VMEM((2, taps, own, half), F32),
            pltpu.VMEM((2, taps, own, half), F32),
            pltpu.VMEM((taps * ch, ch), BF16),
            pltpu.VMEM((taps * ch, ch), BF16),
            pltpu.VMEM((quads * ch, full), BF16),
            pltpu.VMEM((quads * ch, full), BF16),
            pltpu.VMEM((blocks, taps * pair, block), BF16),
            pltpu.VMEM((blocks, taps * pair, block), BF16),
            pltpu.VMEM((blocks, 2 * taps * pair, block), BF16),
            pltpu.VMEM((2, fields, columns, ch), F32),
            pltpu.VMEM((fields, rows + 2, columns + 16, ch), F32),
            pltpu.VMEM((2 * count, taps * ch), BF16),
            pltpu.VMEM((ch // 128, count, 128), F32),
            pltpu.VMEM((2 * small, quads * ch), BF16),
            pltpu.VMEM((chips, small, pair), F32),
            pltpu.VMEM((wide, small, pair), F32),
            pltpu.VMEM((fields, wide + 2, out_cols + 16, pair), F32),
            pltpu.VMEM((fields, 2 * place, taps * pair), BF16),
            pltpu.VMEM((fields * chips, own, place), F32),
            pltpu.VMEM((fields * line, own, place), F32),
            pltpu.VMEM((fields * line, own, place), F32),
            pltpu.VMEM((fields * line, own, place), F32),
            pltpu.VMEM((fields * chips, own, place), F32),
            pltpu.VMEM((fields, taps * pair, place), F32),
            pltpu.VMEM((fields, own, place), F32),
            pltpu.VMEM((fields, own, place), F32),
            dma((5,)), dma((2,)), dma((2,)), dma((2,)), dma((2,)),
            dma((wide,)), dma((wide,)), dma((fields * line,)), dma((fields * line,)),
            dma((fields * line,)), dma((fields * line,)), dma((fields * line,)), dma((fields * line,)),
            dma((fields * chips,)), dma((fields,)), dma((fields,)),
            pltpu.SemaphoreType.REGULAR((max(2, chips - 4),)), pltpu.SemaphoreType.REGULAR((2,)),
        ],
        compiler_params=pltpu.CompilerParams(
            collective_id=0, has_side_effects=True, vmem_limit_bytes=62 << 20
        ),
        cost_estimate=pl.CostEstimate(
            flops=2 * total * taps * full * full // chips, bytes_accessed=12 << 20, transcendentals=0
        ),
    )(features, first, down, inner, outer)


def fits(features, first_weight, down_weight, inner_weight):
    wide = lax.axis_size("wide")
    fields, rows, columns, ch = features.shape
    full = down_weight.shape[3]
    own = full // wide
    return (
        wide % 8 == 0 and rows == 2 and inner_weight.shape[0] == 1 and own % 64 == 0
        and 128 % own == 0 and full % 512 == 0 and ch % 128 == 0 and columns == 16
        and (wide * columns // 2) % 128 == 0 and fields * wide * columns <= 1024
    )


def choose(features, first_weight, down_weight, inner_weight, outer_weight):
    whole = fused_body if fits(features, first_weight, down_weight, inner_weight) else body
    return whole(features, first_weight, down_weight, inner_weight, outer_weight)


def solution(mesh):
    in_specs = (
        P("groups", "wide", None, None),
        P(),
        P(),
        P(None, None, None, None, "wide"),
        P(None, None, None, None, "wide"),
    )
    out_specs = P("groups", None, None, "wide")
    return jax.shard_map(choose, mesh=mesh, in_specs=in_specs, out_specs=out_specs, check_vma=False)
```
